512 devices in a mesh: row: 16 (over x, z_hi), col: 8 (over y), layer: 4 (over z_lo, core).
Axes of the slice: x: 4, y: 8, z: 8 (z_hi: 4, z_lo: 2; z = z_hi * 2 + z_lo), core: 2. Of those that a mesh axis runs over, the one named last changes fastest.
Arguments:
- a_values: float32 [16, 8, 4, 2, 8, 64, 64], P('row', 'col', 'layer'), may hold values from -6 to 6
- a_places: int32 [16, 8, 4, 2, 8, 2], P('row', 'col', 'layer'), may hold values from 0 to 7, as said below
- a_counts: int32 [16, 8, 4, 2], P('row', 'col', 'layer'), may hold values from 2 to 8, as said below
- b_values: float32 [16, 8, 4, 24, 64, 64], P('row', 'col', 'layer'), may hold values from -0.1875 to 0.1875
- b_places: int32 [16, 8, 4, 24, 2], P('row', 'col', 'layer'), may hold values from 0 to 15, as said below
- b_counts: int32 [16, 8, 4], P('row', 'col', 'layer'), may hold values from 6 to 24, as said below
Outputs:
- product: float32 [8192, 8192], P(('row', 'layer'), 'col')
The draws below stay inside these ranges and needn't reach their ends.
Inputs may be any that keep to these rules, and one draw needn't show every extreme that they name: a_places[..., 0] lies below 8 and a_places[..., 1] below 2; within one tile the slots name distinct positions. b_places[..., 0] lies below 2 and b_places[..., 1] below 16; within one tile the slots name distinct positions. `a_counts`: some tile is full. `b_counts`: some tile is full.
All inputs are finite; a program needn't handle non-finite values.
Results may differ from the reference program's by a relative error of at most 0.00007.
Values sent between devices are 32-bit elements; how exact they have to be, the bound alone decides.
No kernel may reach another device: no remote copies, remote signals or barrier semaphores. Data moves between devices by JAX's collectives and lax.ppermute only.
A program may use at most 64 MiB of HBM per device.

```python
import jax
import jax.numpy as jnp
from jax import lax

BLOCK = 64
TILE_ROWS = 8
NBLOCKS = 128
TILE_INNER = 2
TILE_COLS = 16
CYCLE_SLOTS = 2
CAP_A = 8
CAP_B = 24
N_ROW = 16
N_COL = 8
N_LAYER = 4


def distinct_places(key, tiles, rows, cols, capacity):
    total = rows * cols
    scores = jax.random.randint(key, (tiles, total), 0, 65536, dtype=jnp.int32)
    scores = scores * total + jnp.arange(total, dtype=jnp.int32)[None, :]
    order = jnp.argsort(scores, axis=1)[:, :capacity].astype(jnp.int32)
    return jnp.stack([order // cols, order % cols], axis=-1)


def tile_counts(key, tiles, capacity):
    first, second = jax.random.split(key)
    counts = jax.random.randint(first, (tiles,), max(1, capacity // 4), capacity + 1, dtype=jnp.int32)
    chosen = jax.random.randint(second, (), 0, tiles, dtype=jnp.int32)
    return jnp.where(jnp.arange(tiles, dtype=jnp.int32) == chosen, capacity, counts)


def draw_a_places(key, part):
    key = jax.random.fold_in(key, 11)
    tiles = N_ROW * N_COL * N_LAYER * CYCLE_SLOTS
    places = distinct_places(key, tiles, TILE_ROWS, TILE_INNER, CAP_A)
    return places.reshape(N_ROW, N_COL, N_LAYER, CYCLE_SLOTS, CAP_A, 2)


def draw_a_counts(key, part):
    key = jax.random.fold_in(key, 23)
    tiles = N_ROW * N_COL * N_LAYER * CYCLE_SLOTS
    return tile_counts(key, tiles, CAP_A).reshape(N_ROW, N_COL, N_LAYER, CYCLE_SLOTS)


def draw_b_places(key, part):
    key = jax.random.fold_in(key, 37)
    tiles = N_ROW * N_COL * N_LAYER
    places = distinct_places(key, tiles, TILE_INNER, TILE_COLS, CAP_B)
    return places.reshape(N_ROW, N_COL, N_LAYER, CAP_B, 2)


def draw_b_counts(key, part):
    key = jax.random.fold_in(key, 41)
    tiles = N_ROW * N_COL * N_LAYER
    return tile_counts(key, tiles, CAP_B).reshape(N_ROW, N_COL, N_LAYER)


def shard_levels(own_key, extent, cuts, low, high):
    loudness, own = 1.0, jax.random.fold_in(own_key, 6)
    for dim, parts in cuts:
        steps = jnp.exp(jax.random.uniform(jax.random.fold_in(own, dim), (parts,), jnp.float32, low / len(cuts), high / len(cuts)))
        loudness = loudness * jnp.repeat(steps, extent[dim] // parts).reshape([-1 if axis == dim else 1 for axis in range(len(extent))])
    return loudness


def bell_draw(stream_key, extent, scale, limit, cuts=(), held_as=jnp.bfloat16):
    level = shard_levels(stream_key, extent, cuts, -0.22, 0.18) if cuts else 1.0
    array = jax.random.normal(stream_key, extent, jnp.float32) * scale * level
    return jnp.minimum(jnp.maximum(array, -limit), limit).astype(held_as)


def setup_inputs(seed: int = 0) -> dict:
    splits = jax.random.split(jax.random.key(seed), 7)
    a_values = bell_draw(splits[0], (N_ROW, N_COL, N_LAYER, CYCLE_SLOTS, CAP_A, BLOCK, BLOCK), 1.0, 6.0, ((0, 16), (1, 8), (2, 4)), jnp.float32)
    a_places = draw_a_places(jax.random.fold_in(splits[6], 71), 0)
    a_counts = draw_a_counts(jax.random.fold_in(splits[6], 71), 0)
    b_values = bell_draw(splits[3], (N_ROW, N_COL, N_LAYER, CAP_B, BLOCK, BLOCK), (NBLOCKS * BLOCK // 8) ** -0.5, 0.1875, ((0, 16), (1, 8), (2, 4)), jnp.float32)
    b_places = draw_b_places(jax.random.fold_in(splits[6], 71), 0)
    b_counts = draw_b_counts(jax.random.fold_in(splits[6], 71), 0)
    return dict(a_values=a_values, a_places=a_places, a_counts=a_counts, b_values=b_values, b_places=b_places, b_counts=b_counts)


def place_blocks(values, block_rows, block_cols, live):
    zero = jnp.zeros((), values.dtype)
    flat_vals = jnp.where(live[..., None, None], values, zero).reshape(-1, BLOCK, BLOCK)
    grid = jnp.zeros((NBLOCKS, NBLOCKS, BLOCK, BLOCK), values.dtype)
    grid = grid.at[block_rows.reshape(-1), block_cols.reshape(-1)].add(flat_vals)
    return grid.transpose(0, 2, 1, 3).reshape(NBLOCKS * BLOCK, NBLOCKS * BLOCK)


def reference(a_values, a_places, a_counts, b_values, b_places, b_counts):
    row_ids = jnp.arange(N_ROW, dtype=jnp.int32).reshape(-1, 1, 1, 1)
    col_ids = jnp.arange(N_COL, dtype=jnp.int32).reshape(1, -1, 1, 1)
    layer_ids = jnp.arange(N_LAYER, dtype=jnp.int32).reshape(1, 1, -1, 1)
    slot_ids = jnp.arange(CYCLE_SLOTS, dtype=jnp.int32).reshape(1, 1, 1, -1)
    piece_a = N_ROW * layer_ids + (row_ids + col_ids + N_COL * slot_ids) % N_ROW
    rows_a = row_ids[..., None] * TILE_ROWS + a_places[..., 0]
    cols_a = piece_a[..., None] * TILE_INNER + a_places[..., 1]
    live_a = jnp.arange(CAP_A, dtype=jnp.int32) < a_counts[..., None]
    left = place_blocks(a_values, rows_a, cols_a, live_a)
    row_b = row_ids[..., 0]
    col_b = col_ids[..., 0]
    layer_b = layer_ids[..., 0]
    piece_b = N_ROW * layer_b + (row_b + col_b) % N_ROW
    rows_b = piece_b[..., None] * TILE_INNER + b_places[..., 0]
    cols_b = col_b[..., None] * TILE_COLS + b_places[..., 1]
    live_b = jnp.arange(CAP_B, dtype=jnp.int32) < b_counts[..., None]
    right = place_blocks(b_values, rows_b, cols_b, live_b)
    return jnp.dot(left, right, precision=lax.Precision.HIGHEST, preferred_element_type=jnp.float32)
```

```python
import jax
import jax.numpy as jnp
from jax import lax
from jax.experimental import pallas as pl
from jax.experimental.pallas import tpu as pltpu
from jax.sharding import Mesh, PartitionSpec as P

BLOCK = 64
LANES = 128
CAP_A = 8
CAP_B = 24
ROWS_A = 8
INNER = 2
COLS_B = 16
PIECES = 16
B_DATA = CAP_B // 2 * BLOCK
B_ROWS = B_DATA + 8
HALF = B_ROWS // 16 * 8
A_DATA = CAP_A * BLOCK
A_ROWS = A_DATA + 8
WHERE = pl.BlockSpec(memory_space=pl.ANY)
IN_VMEM = pl.BlockSpec(memory_space=pltpu.VMEM)
IN_HBM = pl.BlockSpec(memory_space=pltpu.HBM)
IN_SMEM = pl.BlockSpec(memory_space=pltpu.SMEM)


def around(array, axis, distance):
    n = lax.axis_size(axis)
    return lax.ppermute(array, axis, [(i, (i + distance) % n) for i in range(n)])


def slot_at(places, count, cols, base):
    slots = places.shape[1]
    spot = places[0:1, :] * cols + places[1:2, :] + base
    position = lax.broadcasted_iota(jnp.int32, (LANES, slots), 0)
    slot = lax.broadcasted_iota(jnp.int32, (LANES, slots), 1)
    hit = (position == spot) & (slot < count)
    return jnp.max(jnp.where(hit, slot + 1, 0), axis=1, keepdims=True)


def as_rows(column):
    return jnp.transpose(jnp.broadcast_to(column.astype(jnp.float32), (LANES, LANES)))[0:8, :]


def pack_kernel(*refs):
    ins, (a_ref, b_ref), held, sems = refs[:6], refs[6:8], refs[8:14], refs[14]
    an_ref, bn_ref, ap_ref, bp_ref, bv_ref, av_ref = held
    copies = [pltpu.make_async_copy(ins[k], held[k], sems.at[k]) for k in range(6)]
    for copy in copies:
        copy.start()
    for copy in copies[:4]:
        copy.wait()
    copy_b, copy_a = copies[4:]
    spots = slot_at(ap_ref[0], an_ref[0], INNER, 0) + slot_at(ap_ref[1], an_ref[1], INNER, 16) - 1
    a_ref[A_DATA:, :] = as_rows(spots)
    spots = slot_at(bp_ref[...], bn_ref[0], COLS_B, 0) - 1
    b_ref[B_DATA:, :] = as_rows(spots)
    copy_b.wait()
    for pair in range(CAP_B // 2):
        b_ref[pair * BLOCK : (pair + 1) * BLOCK, :] = jnp.concatenate(
            [bv_ref[2 * pair], bv_ref[2 * pair + 1]], axis=1
        )
    copy_a.wait()
    for pair in range(CAP_A):
        a_ref[pair * BLOCK : (pair + 1) * BLOCK, :] = jnp.concatenate(
            [av_ref[2 * pair], av_ref[2 * pair + 1]], axis=1
        )


def pack(an, bn, ap, bp, bv, av):
    return pl.pallas_call(
        pack_kernel,
        out_shape=(
            jax.ShapeDtypeStruct((A_ROWS, LANES), jnp.float32),
            jax.ShapeDtypeStruct((B_ROWS, LANES), jnp.float32),
        ),
        in_specs=[IN_HBM] * 6,
        out_specs=(IN_VMEM, IN_VMEM),
        scratch_shapes=[
            pltpu.SMEM(an.shape, jnp.int32),
            pltpu.SMEM(bn.shape, jnp.int32),
            pltpu.VMEM(ap.shape, jnp.int32),
            pltpu.VMEM(bp.shape, jnp.int32),
            pltpu.VMEM(bv.shape, jnp.float32),
            pltpu.VMEM(av.shape, jnp.float32),
            pltpu.SemaphoreType.DMA((6,)),
        ],
        compiler_params=pltpu.CompilerParams(vmem_limit_bytes=56 * 1024 * 1024),
    )(an, bn, ap, bp, bv, av)


LAST = B_ROWS - HALF
PIECE_LIST = (
    [(0, 0, B_ROWS, 0, 0), (1, 0, B_ROWS, 4, 0), (2, 0, B_ROWS, 8, 0), (3, 0, B_ROWS, 1, 0), (4, 0, B_ROWS, 2, 0)]
    + [(5, 0, HALF, 12, 0), (6, 0, LAST, 12, HALF)]
    + [(7, 0, B_ROWS, 5, 0), (7, B_ROWS, B_ROWS, 9, 0), (7, 2 * B_ROWS, HALF, 3, 0)]
    + [(8, 0, B_ROWS, 6, 0), (8, B_ROWS, B_ROWS, 10, 0), (8, 2 * B_ROWS, LAST, 3, HALF)]
    + [(9, 0, B_ROWS, 13, 0), (9, B_ROWS, B_ROWS, 7, 0)]
    + [(10, 0, B_ROWS, 14, 0), (10, B_ROWS, B_ROWS, 11, 0)]
    + [(11, 0, HALF, 15, 0), (12, 0, LAST, 15, HALF)]
)
CALLS = ((0, 1, 2, 4, 8, 3, 12, 5, 6, 9, 10), (13, 14, 7, 11), (15,))
ORDER = sum(CALLS, ())


def block_pair(load, left, right):
    lane = lax.broadcasted_iota(jnp.int32, (BLOCK, LANES), 1)
    low = jnp.maximum(left, 0)
    high = jnp.maximum(right, 0)
    one = pltpu.roll(load(low // 2), (low % 2) * BLOCK, 1)
    two = pltpu.roll(load(high // 2), (1 - high % 2) * BLOCK, 1)
    one = jnp.where((lane < BLOCK) & (left >= 0), one, 0.0)
    return jnp.where((lane >= BLOCK) & (right >= 0), two, one)


def halves(value):
    top = value.astype(jnp.bfloat16)
    return top, (value - top.astype(jnp.float32)).astype(jnp.bfloat16)


def place_left(me_ref, a_f, spots_s, a_hi, a_lo):
    x, zh, col, zl, core = (me_ref[k] for k in range(5))

    def left_tile(index, _):
        source = index // 2
        slot = index % 2
        owner = (4 * x + zh + source + 8 * slot - col) % PIECES
        off_x = (owner // 4 + 4 - x) % 4
        off_z = (owner % 4 + 4 - zh) % 4
        dx = jnp.where(off_x == 0, 0, jnp.where(off_x == 3, 1, off_x + 1))
        dz = jnp.where(off_z == 0, 0, jnp.where(off_z == 3, 1, off_z + 1))
        at = me_ref[5 + 4 * dz + dx]
        lanes = pl.ds(pl.multiple_of(at * LANES, LANES), LANES)
        for r in range(ROWS_A):
            quarter = r // 2
            place = jnp.where(quarter % 2 == core, 2, 0) + jnp.where(quarter // 2 == zl, 1, 0)
            rows = pl.ds(pl.multiple_of(place * 128 + (r % 2) * BLOCK, BLOCK), BLOCK)

            def load(pair):
                return a_f[source, pl.ds(pl.multiple_of((slot * 4 + pair) * BLOCK, BLOCK), BLOCK), :]

            left = spots_s[source, slot * 16 + 2 * r].astype(jnp.int32)
            right = spots_s[source, slot * 16 + 2 * r + 1].astype(jnp.int32)
            a_hi[rows, lanes], a_lo[rows, lanes] = halves(block_pair(load, left, right))
        return 0

    lax.fori_loop(0, 16, left_tile, 0)


def right_copies(call, b_in, b_f, spots_s, sem_b, sem_s):
    tiles = CALLS[call]
    copies, spots = [], []
    used = sorted({piece[0] for piece in PIECE_LIST if piece[3] in tiles})
    for operand, first, rows, tile, at in PIECE_LIST:
        if tile not in tiles:
            continue
        source, index = b_in[used.index(operand)], tiles.index(tile)
        copies.append(
            pltpu.make_async_copy(
                source.at[pl.ds(first, rows)], b_f.at[index, pl.ds(at, rows)], sem_b.at[len(copies)]
            )
        )
        if at <= B_DATA < at + rows:
            row = first + B_DATA - at
            spots.append(pltpu.make_async_copy(source.at[row], spots_s.at[index], sem_s.at[index]))
    return copies, spots


def place_right(tiles, b_f, spots_s, b_hi, b_lo):
    def right_tile(tile, _):
        for k in range(INNER):
            rows = pl.ds(pl.multiple_of(tile * LANES + k * BLOCK, BLOCK), BLOCK)
            for c in range(COLS_B // 2):

                def load(pair):
                    return b_f[tile, pl.ds(pl.multiple_of(pair * BLOCK, BLOCK), BLOCK), :]

                spot = k * COLS_B + 2 * c
                left = spots_s[tile, spot].astype(jnp.int32)
                right = spots_s[tile, spot + 1].astype(jnp.int32)
                lanes = slice(c * LANES, (c + 1) * LANES)
                b_hi[rows, lanes], b_lo[rows, lanes] = halves(block_pair(load, left, right))
        return 0

    lax.fori_loop(0, tiles, right_tile, 0)


def partial_product(call, a_hi, a_lo, b_hi, b_lo, store):
    first = sum(len(tiles) for tiles in CALLS[:call]) * LANES
    depth = len(CALLS[call]) * LANES
    left_hi, left_lo = a_hi[:, first : first + depth], a_lo[:, first : first + depth]
    for n in range(4):
        lanes = slice(n * 256, (n + 1) * 256)
        top = b_hi[:, lanes]
        total = jnp.dot(left_lo, top, preferred_element_type=jnp.float32)
        total += jnp.dot(left_hi, b_lo[:, lanes], preferred_element_type=jnp.float32)
        total += jnp.dot(left_hi, top, preferred_element_type=jnp.float32)
        store(lanes, total)


def first_kernel(n_right, *refs):
    me_ref, a_in = refs[0], refs[1]
    b_in = refs[2 : 2 + n_right]
    a_hi, a_lo, c_ref = refs[2 + n_right : 5 + n_right]
    a_f, spots_a, sem_a, sem_sa, b_f, b_hi, b_lo, spots_b, sem_b, sem_s = refs[5 + n_right :]
    copy_a = pltpu.make_async_copy(a_in, a_f, sem_a)
    copies, spots = right_copies(0, b_in, b_f, spots_b, sem_b, sem_s)
    copy_a.start()
    spots_of_a = [pltpu.make_async_copy(a_in.at[k, A_DATA], spots_a.at[k], sem_sa.at[k]) for k in range(8)]
    for copy in spots_of_a + spots + copies:
        copy.start()
    for copy in spots_of_a + [copy_a]:
        copy.wait()
    place_left(me_ref, a_f, spots_a, a_hi, a_lo)
    for copy in spots + copies:
        copy.wait()
    place_right(len(CALLS[0]), b_f, spots_b, b_hi, b_lo)

    def store(lanes, total):
        c_ref[:, lanes] = total

    partial_product(0, a_hi, a_lo, b_hi, b_lo, store)


def later_kernel(call, n_right, *refs):
    a_hi, a_lo, c_in = refs[:3]
    b_in = refs[3 : 3 + n_right]
    rest = refs[3 + n_right :]
    outs, (b_f, b_hi, b_lo, spots_b, sem_b, sem_s) = rest[:-6], rest[-6:]
    copies, spots = right_copies(call, b_in, b_f, spots_b, sem_b, sem_s)
    for copy in spots + copies:
        copy.start()
    for copy in spots + copies:
        copy.wait()
    place_right(len(CALLS[call]), b_f, spots_b, b_hi, b_lo)

    def store(lanes, total):
        total += c_in[:, lanes]
        if call == 1:
            outs[0][:, lanes] = total
        else:
            outs[0][:, lanes] = total[:256]
            outs[1][:, lanes] = total[256:384]
            outs[2][:, lanes] = total[384:]

    partial_product(call, a_hi, a_lo, b_hi, b_lo, store)


def right_scratch(call):
    tiles = len(CALLS[call])
    copies = sum(piece[3] in CALLS[call] for piece in PIECE_LIST)
    return [
        pltpu.VMEM((tiles, B_ROWS, LANES), jnp.float32),
        pltpu.VMEM((tiles * LANES, 1024), jnp.bfloat16),
        pltpu.VMEM((tiles * LANES, 1024), jnp.bfloat16),
        pltpu.SMEM((tiles, LANES), jnp.float32),
        pltpu.SemaphoreType.DMA((copies,)),
        pltpu.SemaphoreType.DMA((tiles,)),
    ]


def used_by(call, b_all):
    return [b_all[k] for k in sorted({piece[0] for piece in PIECE_LIST if piece[3] in CALLS[call]})]


def cost(call):
    flops = 3 * 2 * 512 * 1024 * LANES * len(CALLS[call])
    return pl.CostEstimate(flops=flops, bytes_accessed=16 * 1024 * 1024, transcendentals=0)


def first_product(me, a_all, b_all):
    operands = used_by(0, b_all)
    depth = PIECES * LANES
    return pl.pallas_call(
        lambda *refs: first_kernel(len(operands), *refs),
        out_shape=(
            jax.ShapeDtypeStruct((512, depth), jnp.bfloat16),
            jax.ShapeDtypeStruct((512, depth), jnp.bfloat16),
            jax.ShapeDtypeStruct((512, 1024), jnp.float32),
        ),
        in_specs=[IN_SMEM] + [WHERE] * (1 + len(operands)),
        out_specs=(IN_VMEM, IN_VMEM, IN_VMEM),
        scratch_shapes=[
            pltpu.VMEM((8, A_ROWS, LANES), jnp.float32),
            pltpu.SMEM((8, LANES), jnp.float32),
            pltpu.SemaphoreType.DMA,
            pltpu.SemaphoreType.DMA((8,)),
        ]
        + right_scratch(0),
        compiler_params=pltpu.CompilerParams(vmem_limit_bytes=28 * 1024 * 1024),
        cost_estimate=cost(0),
    )(me, a_all, *operands)


def later_product(call, a_hi, a_lo, so_far, b_all):
    operands = used_by(call, b_all)
    shapes = ((512, 1024),) if call == 1 else ((256, 1024), (128, 1024), (128, 1024))
    return pl.pallas_call(
        lambda *refs: later_kernel(call, len(operands), *refs),
        out_shape=tuple(jax.ShapeDtypeStruct(shape, jnp.float32) for shape in shapes),
        in_specs=[IN_VMEM] * 3 + [WHERE] * len(operands),
        out_specs=(IN_VMEM,) * len(shapes),
        scratch_shapes=right_scratch(call),
        compiler_params=pltpu.CompilerParams(vmem_limit_bytes=20 * 1024 * 1024),
        cost_estimate=cost(call),
    )(a_hi, a_lo, so_far, *operands)


def body(a_values, a_places, a_counts, b_values, b_places, b_counts):
    hold = lax.optimization_barrier
    me = [lax.axis_index(name) for name in ("x", "zh", "col", "zl", "core")]
    me = jnp.stack(me + [ORDER.index(tile) for tile in range(PIECES)]).astype(jnp.int32)
    own_a, own = pack(
        a_counts.reshape(2),
        b_counts.reshape(1),
        a_places.reshape(2, CAP_A, 2).swapaxes(1, 2),
        b_places.reshape(CAP_B, 2).swapaxes(0, 1),
        b_values.reshape(CAP_B, BLOCK, BLOCK),
        a_values.reshape(2 * CAP_A, BLOCK, BLOCK),
    )
    a_all = lax.all_gather(own_a, "col")

    z_behind = around(own, "zh", 1)
    z_ahead = around(own, "zh", -1)
    x_behind = around(own, "x", 1)
    x_ahead = around(own, "x", -1)
    z_behind, z_ahead, x_behind, x_ahead = hold((z_behind, z_ahead, x_behind, x_ahead))

    z_far0 = around(z_behind[:HALF], "zh", 1)
    z_far1 = around(z_ahead[HALF:], "zh", -1)
    two_behind = around(jnp.concatenate([z_behind, z_ahead, x_behind[:HALF]], axis=0), "x", 1)
    two_ahead = around(jnp.concatenate([z_behind, z_ahead, x_ahead[HALF:]], axis=0), "x", -1)
    z_far0, z_far1, two_behind, two_ahead = hold((z_far0, z_far1, two_behind, two_ahead))

    three_behind = around(jnp.concatenate([z_far0, z_far1, two_behind[:B_ROWS]], axis=0), "x", 1)
    three_ahead = around(jnp.concatenate([z_far0, z_far1, two_ahead[B_ROWS : 2 * B_ROWS]], axis=0), "x", -1)
    b_all = [own, z_behind, z_ahead, x_behind, x_ahead, z_far0, z_far1, two_behind, two_ahead]
    a_hi, a_lo, total = first_product(me, a_all, b_all)
    three_behind, three_ahead, a_hi, a_lo, total = hold((three_behind, three_ahead, a_hi, a_lo, total))

    four_behind = around(three_behind[:HALF], "x", 1)
    four_ahead = around(three_ahead[HALF:B_ROWS], "x", -1)
    b_all += [three_behind, three_ahead, four_behind, four_ahead]
    (total,) = later_product(1, a_hi, a_lo, total, b_all)
    other, send, keep = later_product(2, a_hi, a_lo, total, b_all)

    got = around(other, "core", 1)
    ahead = around(send + got[:128], "zl", 1)
    return (keep + got[128:]) + ahead


def solution(mesh):
    split = Mesh(mesh.devices.reshape(4, 4, 8, 2, 2), ("x", "zh", "col", "zl", "core"))
    row, layer = ("x", "zh"), ("zl", "core")
    in_specs = (
        P(row, "col", layer, None, None, None, None),
        P(row, "col", layer, None, None, None),
        P(row, "col", layer, None),
        P(row, "col", layer, None, None, None),
        P(row, "col", layer, None, None),
        P(row, "col", layer),
    )
    out_specs = P(("x", "zh", "zl", "core"), "col")
    return jax.shard_map(body, mesh=split, in_specs=in_specs, out_specs=out_specs, check_vma=False)
```

```python
import jax
import jax.numpy as jnp
from jax import lax
from jax.experimental import pallas as pl
from jax.experimental.pallas import tpu as pltpu
from jax.sharding import Mesh, PartitionSpec as P

BLOCK = 64
LANES = 128
CAP_A = 8
CAP_B = 24
ROWS_A = 8
INNER = 2
COLS_B = 16
PIECES = 16
B_DATA = CAP_B // 2 * BLOCK
B_ROWS = B_DATA + 8
A_DATA = CAP_A * BLOCK
A_ROWS = A_DATA + 8
WHERE = pl.BlockSpec(memory_space=pl.ANY)
IN_VMEM = pl.BlockSpec(memory_space=pltpu.VMEM)
BIG = 56 * 1024 * 1024
EARLY = 20 * 1024 * 1024
FIRST = 20 * 1024 * 1024
IN_HBM = pl.BlockSpec(memory_space=pltpu.HBM)
IN_SMEM = pl.BlockSpec(memory_space=pltpu.SMEM)


def exchange(array, axis, step):
    mask = {0: (1, 3)[step], 1: (3, 1)[step]}
    route = [(2 * i + core, 2 * (i ^ mask[core]) + core) for i in range(4) for core in range(2)]
    return lax.ppermute(array, (axis, "core"), route)


def col_partner(place, core, distance):
    if distance == 4:
        return place ^ 4
    if distance == 2:
        forward = place // 2 % 2 == (core + place) % 2
        return (place + (2 if forward else -2)) % 8
    return (place + (1 if place % 2 == core else -1)) % 8


def exchange_col(array, distance):
    route = [(2 * i + core, 2 * col_partner(i, core, distance) + core) for i in range(8) for core in range(2)]
    return lax.ppermute(array, ("col", "core"), route)


def holders(place, core):
    held = [place]
    for distance in (4, 2, 1):
        partner = holders_before(col_partner(place, core, distance), core, distance)
        held = held + partner
    return held


def holders_before(place, core, distance):
    held = [place]
    for earlier in (4, 2):
        if earlier <= distance:
            break
        held = held + holders_before(col_partner(place, core, earlier), core, earlier)
    return held


def swap(array, axis):
    return lax.ppermute(array, axis, [(0, 1), (1, 0)])


def slot_at(places, count, cols, base):
    slots = places.shape[1]
    spot = places[0:1, :] * cols + places[1:2, :] + base
    position = lax.broadcasted_iota(jnp.int32, (LANES, slots), 0)
    slot = lax.broadcasted_iota(jnp.int32, (LANES, slots), 1)
    hit = (position == spot) & (slot < count)
    return jnp.max(jnp.where(hit, slot + 1, 0), axis=1, keepdims=True)


def as_rows(column):
    return jnp.transpose(jnp.broadcast_to(column.astype(jnp.float32), (LANES, LANES)))[0:8, :]


def pack_kernel(*refs):
    ins, (a_ref, b_ref), held, sems = refs[:6], refs[6:8], refs[8:14], refs[14]
    an_ref, bn_ref, ap_ref, bp_ref, bv_ref, av_ref = held
    copies = [pltpu.make_async_copy(ins[k], held[k], sems.at[k]) for k in range(6)]
    for copy in copies:
        copy.start()
    for copy in copies[:4]:
        copy.wait()
    copy_b, copy_a = copies[4:]
    spots = slot_at(ap_ref[0], an_ref[0], INNER, 0) + slot_at(ap_ref[1], an_ref[1], INNER, 16) - 1
    a_ref[A_DATA:, :] = as_rows(spots)
    spots = slot_at(bp_ref[...], bn_ref[0, 0, 0], COLS_B, 0) - 1
    b_ref[B_DATA:, :] = as_rows(spots)
    copy_b.wait()
    for pair in range(CAP_B // 2):
        b_ref[pair * BLOCK : (pair + 1) * BLOCK, :] = jnp.concatenate(
            [bv_ref[2 * pair], bv_ref[2 * pair + 1]], axis=1
        )
    copy_a.wait()
    for pair in range(CAP_A):
        a_ref[pair * BLOCK : (pair + 1) * BLOCK, :] = jnp.concatenate(
            [av_ref[2 * pair], av_ref[2 * pair + 1]], axis=1
        )


def pack(an, bn, ap, bp, bv, av):
    return pl.pallas_call(
        pack_kernel,
        out_shape=(
            jax.ShapeDtypeStruct((A_ROWS, LANES), jnp.float32),
            jax.ShapeDtypeStruct((B_ROWS, LANES), jnp.float32),
        ),
        in_specs=[IN_HBM] * 6,
        out_specs=(IN_VMEM, IN_VMEM),
        scratch_shapes=[
            pltpu.SMEM(an.shape, jnp.int32),
            pltpu.SMEM(bn.shape, jnp.int32),
            pltpu.VMEM(ap.shape, jnp.int32),
            pltpu.VMEM(bp.shape, jnp.int32),
            pltpu.VMEM(bv.shape, jnp.float32),
            pltpu.VMEM(av.shape, jnp.float32),
            pltpu.SemaphoreType.DMA((6,)),
        ],
        compiler_params=pltpu.CompilerParams(vmem_limit_bytes=BIG),
    )(an, bn, ap, bp, bv, av)


HELD = ((0,), (4,), (1,), (8, 12), (2, 3), (5, 9, 13), (6, 10, 14), (7, 11, 15))
CALLS = ((0, 4, 1, 8, 12, 2, 3), (5, 9, 13, 6, 10, 14), (7, 11, 15))
ORDER = sum(CALLS, ())


def block_pair(load, left, right):
    lane = lax.broadcasted_iota(jnp.int32, (BLOCK, LANES), 1)
    low = jnp.maximum(left, 0)
    high = jnp.maximum(right, 0)
    one = pltpu.roll(load(low // 2), (low % 2) * BLOCK, 1)
    two = pltpu.roll(load(high // 2), (1 - high % 2) * BLOCK, 1)
    one = jnp.where((lane < BLOCK) & (left >= 0), one, 0.0)
    return jnp.where((lane >= BLOCK) & (right >= 0), two, one)


def halves(value):
    top = value.astype(jnp.bfloat16)
    return top, (value - top.astype(jnp.float32)).astype(jnp.bfloat16)


def ring_place(mask, core):
    near = jnp.where(mask == 1 + 2 * core, 1, 2)
    return jnp.where(mask == 0, 0, jnp.where(mask == 2, 3, near))


def place_left(me_ref, a_f, spots_s, a_hi, a_lo):
    x, zh, col, zl, core = (me_ref[k] for k in range(5))

    def left_tile(index, _):
        source = index // 2
        slot = index % 2
        holder = me_ref[5 + PIECES + (2 * col + core) * 8 + source]
        owner = (4 * x + zh + holder + 8 * slot + PIECES - col) % PIECES
        dx = ring_place((owner // 4) ^ x, core)
        dz = ring_place((owner % 4) ^ zh, core)
        at = me_ref[5 + 4 * dz + dx]
        lanes = pl.ds(pl.multiple_of(at * LANES, LANES), LANES)
        for r in range(ROWS_A):
            quarter = r // 2
            place = jnp.where(quarter % 2 == core, 2, 0) + jnp.where(quarter // 2 == zl, 1, 0)
            rows = pl.ds(pl.multiple_of(place * 128 + (r % 2) * BLOCK, BLOCK), BLOCK)

            def load(pair):
                return a_f[source, pl.ds(pl.multiple_of((slot * 4 + pair) * BLOCK, BLOCK), BLOCK), :]

            left = spots_s[source, slot * 16 + 2 * r].astype(jnp.int32)
            right = spots_s[source, slot * 16 + 2 * r + 1].astype(jnp.int32)
            a_hi[rows, lanes], a_lo[rows, lanes] = halves(block_pair(load, left, right))
        return 0

    lax.fori_loop(0, 16, left_tile, 0)


def right_copies(call, b_in, b_f, spots_s, sem_b, sem_s):
    tiles = CALLS[call]
    copies, spots = [], []
    for source, held in zip(b_in, [held for held in HELD if held[0] in tiles], strict=True):
        for k, tile in enumerate(held):
            at = tiles.index(tile)
            rows = pl.ds(k * B_ROWS, B_ROWS)
            copies.append(pltpu.make_async_copy(source.at[rows], b_f.at[at], sem_b.at[at]))
            spots.append(pltpu.make_async_copy(source.at[k * B_ROWS + B_DATA], spots_s.at[at], sem_s.at[at]))
    return copies, spots


def place_right(tiles, b_f, spots_s, b_hi, b_lo):
    def right_tile(tile, _):
        for k in range(INNER):
            rows = pl.ds(pl.multiple_of(tile * LANES + k * BLOCK, BLOCK), BLOCK)
            for c in range(COLS_B // 2):

                def load(pair):
                    return b_f[tile, pl.ds(pl.multiple_of(pair * BLOCK, BLOCK), BLOCK), :]

                spot = k * COLS_B + 2 * c
                left = spots_s[tile, spot].astype(jnp.int32)
                right = spots_s[tile, spot + 1].astype(jnp.int32)
                lanes = slice(c * LANES, (c + 1) * LANES)
                b_hi[rows, lanes], b_lo[rows, lanes] = halves(block_pair(load, left, right))
        return 0

    lax.fori_loop(0, tiles, right_tile, 0)


def first_lane(call):
    return sum(len(tiles) for tiles in CALLS[:call]) * LANES


def partial_product(left_hi, left_lo, b_hi, b_lo, store):
    for n in range(4):
        lanes = slice(n * 256, (n + 1) * 256)
        top = b_hi[:, lanes]
        total = jnp.dot(left_lo, top, preferred_element_type=jnp.float32)
        total += jnp.dot(left_hi, b_lo[:, lanes], preferred_element_type=jnp.float32)
        total += jnp.dot(left_hi, top, preferred_element_type=jnp.float32)
        store(lanes, total)


def early_kernel(n_right, *refs):
    b_in = refs[:n_right]
    b_hi, b_lo, b_f, spots_b, sem_b, sem_s = refs[n_right:]
    copies, spots = right_copies(0, b_in, b_f, spots_b, sem_b, sem_s)
    for copy in spots + copies:
        copy.start()
    for copy in spots + copies:
        copy.wait()
    place_right(len(CALLS[0]), b_f, spots_b, b_hi, b_lo)


def first_kernel(*refs):
    me_ref, a_in, b_in = refs[0], refs[1:5], refs[5:7]
    a_hi, a_lo, c_ref = refs[7:10]
    a_f, spots_a, sem_a, sem_sa, b_hi, b_lo, sem_b = refs[10:]
    parts = [(part, k) for part in a_in for k in range(part.shape[0] // A_ROWS)]
    copies_a, spots_of_a = [], []
    for n, (part, k) in enumerate(parts):
        rows = pl.ds(k * A_ROWS, A_ROWS)
        copies_a.append(pltpu.make_async_copy(part.at[rows], a_f.at[n], sem_a.at[n]))
        spots_of_a.append(pltpu.make_async_copy(part.at[k * A_ROWS + A_DATA], spots_a.at[n], sem_sa.at[n]))
    copies = [pltpu.make_async_copy(b_in[k], (b_hi, b_lo)[k], sem_b.at[k]) for k in range(2)]
    for copy in spots_of_a + copies_a + copies:
        copy.start()
    for copy in spots_of_a + copies_a:
        copy.wait()
    place_left(me_ref, a_f, spots_a, a_hi, a_lo)
    for copy in copies:
        copy.wait()

    def store(lanes, total):
        c_ref[:, lanes] = total

    depth = len(CALLS[0]) * LANES
    partial_product(a_hi[:, :depth], a_lo[:, :depth], b_hi, b_lo, store)


def middle_kernel(call, n_right, *refs):
    a_in, c_in = refs[:2], refs[2]
    b_in = refs[3 : 3 + n_right]
    c_out, a_hi, a_lo, c_held, sem_a, b_f, b_hi, b_lo, spots_b, sem_b, sem_s = refs[3 + n_right :]
    copies, spots = right_copies(call, b_in, b_f, spots_b, sem_b, sem_s)
    lanes = pl.ds(first_lane(call), len(CALLS[call]) * LANES)
    held = [pltpu.make_async_copy(a_in[k].at[:, lanes], (a_hi, a_lo)[k], sem_a.at[k]) for k in range(2)]
    held.append(pltpu.make_async_copy(c_in, c_held, sem_a.at[2]))
    for copy in spots + copies + held:
        copy.start()
    for copy in spots + copies:
        copy.wait()
    place_right(len(CALLS[call]), b_f, spots_b, b_hi, b_lo)
    for copy in held:
        copy.wait()

    def store(lanes, total):
        c_out[:, lanes] = total + c_held[:, lanes]

    partial_product(a_hi[...], a_lo[...], b_hi, b_lo, store)


def last_kernel(call, n_right, *refs):
    a_hi, a_lo, c_in = refs[:3]
    b_in = refs[3 : 3 + n_right]
    other, send, keep, b_f, b_hi, b_lo, spots_b, sem_b, sem_s = refs[3 + n_right :]
    copies, spots = right_copies(call, b_in, b_f, spots_b, sem_b, sem_s)
    for copy in spots + copies:
        copy.start()
    for copy in spots + copies:
        copy.wait()
    place_right(len(CALLS[call]), b_f, spots_b, b_hi, b_lo)

    def store(lanes, total):
        total += c_in[:, lanes]
        other[:, lanes] = total[:256]
        send[:, lanes] = total[256:384]
        keep[:, lanes] = total[384:]

    first = first_lane(call)
    depth = len(CALLS[call]) * LANES
    partial_product(a_hi[:, first : first + depth], a_lo[:, first : first + depth], b_hi, b_lo, store)


def right_scratch(call):
    tiles = len(CALLS[call])
    return [
        pltpu.VMEM((tiles, B_ROWS, LANES), jnp.float32),
        pltpu.VMEM((tiles * LANES, 1024), jnp.bfloat16),
        pltpu.VMEM((tiles * LANES, 1024), jnp.bfloat16),
        pltpu.SMEM((tiles, LANES), jnp.float32),
        pltpu.SemaphoreType.DMA((tiles,)),
        pltpu.SemaphoreType.DMA((tiles,)),
    ]


def used_by(call, b_all):
    return [b_all[k] for k in range(len(HELD)) if HELD[k][0] in CALLS[call]]


def cost(call):
    flops = 3 * 2 * 512 * 1024 * LANES * len(CALLS[call])
    return pl.CostEstimate(flops=flops, bytes_accessed=16 * 1024 * 1024, transcendentals=0)


def early_right(b_all):
    operands = used_by(0, b_all)
    depth = len(CALLS[0]) * LANES
    scratch = right_scratch(0)
    return pl.pallas_call(
        lambda *refs: early_kernel(len(operands), *refs),
        out_shape=(jax.ShapeDtypeStruct((depth, 1024), jnp.bfloat16),) * 2,
        in_specs=[WHERE] * len(operands),
        out_specs=(IN_VMEM,) * 2,
        scratch_shapes=scratch[:1] + scratch[3:],
        compiler_params=pltpu.CompilerParams(vmem_limit_bytes=EARLY),
        cost_estimate=pl.CostEstimate(flops=10**9, bytes_accessed=16 * 1024 * 1024, transcendentals=0),
    )(*operands)


def first_product(me, a_all, right):
    depth = PIECES * LANES
    return pl.pallas_call(
        first_kernel,
        out_shape=(
            jax.ShapeDtypeStruct((512, depth), jnp.bfloat16),
            jax.ShapeDtypeStruct((512, depth), jnp.bfloat16),
            jax.ShapeDtypeStruct((512, 1024), jnp.float32),
        ),
        in_specs=[IN_SMEM] + [WHERE] * 6,
        out_specs=(IN_VMEM,) * 3,
        scratch_shapes=[
            pltpu.VMEM((8, A_ROWS, LANES), jnp.float32),
            pltpu.SMEM((8, LANES), jnp.float32),
            pltpu.SemaphoreType.DMA((8,)),
            pltpu.SemaphoreType.DMA((8,)),
        ]
        + right_scratch(0)[1:3]
        + [pltpu.SemaphoreType.DMA((2,))],
        compiler_params=pltpu.CompilerParams(vmem_limit_bytes=FIRST),
        cost_estimate=cost(0),
    )(me, *a_all, *right)


def middle_product(call, a_hi, a_lo, so_far, b_all, limit):
    operands = used_by(call, b_all)
    depth = len(CALLS[call]) * LANES
    return pl.pallas_call(
        lambda *refs: middle_kernel(call, len(operands), *refs),
        out_shape=jax.ShapeDtypeStruct((512, 1024), jnp.float32),
        in_specs=[WHERE] * (3 + len(operands)),
        out_specs=IN_VMEM,
        scratch_shapes=[
            pltpu.VMEM((512, depth), jnp.bfloat16),
            pltpu.VMEM((512, depth), jnp.bfloat16),
            pltpu.VMEM((512, 1024), jnp.float32),
            pltpu.SemaphoreType.DMA((3,)),
        ]
        + right_scratch(call),
        compiler_params=pltpu.CompilerParams(vmem_limit_bytes=limit),
        cost_estimate=cost(call),
    )(a_hi, a_lo, so_far, *operands)


def last_product(call, a_hi, a_lo, so_far, b_all):
    operands = used_by(call, b_all)
    return pl.pallas_call(
        lambda *refs: last_kernel(call, len(operands), *refs),
        out_shape=tuple(jax.ShapeDtypeStruct((rows, 1024), jnp.float32) for rows in (256, 128, 128)),
        in_specs=[IN_VMEM] * 3 + [WHERE] * len(operands),
        out_specs=(IN_VMEM,) * 3,
        scratch_shapes=right_scratch(call),
        compiler_params=pltpu.CompilerParams(vmem_limit_bytes=16 * 1024 * 1024),
        cost_estimate=cost(call),
    )(a_hi, a_lo, so_far, *operands)


def body(a_values, a_places, a_counts, b_values, b_places, b_counts):
    hold = lax.optimization_barrier
    by_place = [holder for place in range(8) for core in range(2) for holder in holders(place, core)]
    me = [lax.axis_index(name) for name in ("x", "zh", "col", "zl", "core")]
    table = jnp.array([ORDER.index(tile) for tile in range(PIECES)] + by_place, jnp.int32)
    me = jnp.concatenate([jnp.stack(me).astype(jnp.int32), table])
    own_a, own = pack(
        a_counts.reshape(2),
        b_counts,
        a_places.reshape(2, CAP_A, 2).swapaxes(1, 2),
        b_places.reshape(CAP_B, 2).swapaxes(0, 1),
        b_values.reshape(CAP_B, BLOCK, BLOCK),
        a_values.reshape(2 * CAP_A, BLOCK, BLOCK),
    )
    z_one = exchange(own, "zh", 0)
    x_one = exchange(own, "x", 0)
    a_one = exchange_col(own_a, 4)
    z_one, x_one, a_one = hold((z_one, x_one, a_one))

    z_two = exchange(jnp.concatenate([own, z_one], axis=0), "zh", 1)
    x_two = exchange(jnp.concatenate([own, x_one], axis=0), "x", 1)
    a_two = exchange_col(jnp.concatenate([own_a, a_one], axis=0), 2)
    z_two, x_two = hold((z_two, x_two))

    column = jnp.concatenate([z_one, z_two], axis=0)
    x_three = exchange(column, "x", 0)
    x_four = exchange(column, "x", 1)
    b_all = [own, z_one, x_one, z_two, x_two]
    x_two, a_two = hold((x_two, a_two))
    b_all = [own, z_one, x_one, z_two, x_two]
    right_hi, right_lo = early_right(b_all)
    a_two, right_hi, right_lo = hold((a_two, right_hi, right_lo))
    a_four = exchange_col(jnp.concatenate([own_a, a_one, a_two], axis=0), 1)
    a_hi, a_lo, total = first_product(me, (own_a, a_one, a_two, a_four), (right_hi, right_lo))

    b_all += [x_three, x_four, exchange(x_three, "x", 1)]
    total = middle_product(1, a_hi, a_lo, total, b_all, 20 * 1024 * 1024)
    other, send, keep = last_product(2, a_hi, a_lo, total, b_all)

    got = swap(other, "core")
    ahead = swap(send + got[:128], "zl")
    return (keep + got[128:]) + ahead


def solution(mesh):
    split = Mesh(mesh.devices.reshape(4, 4, 8, 2, 2), ("x", "zh", "col", "zl", "core"))
    row, layer = ("x", "zh"), ("zl", "core")
    in_specs = (
        P(row, "col", layer, None, None, None, None),
        P(row, "col", layer, None, None, None),
        P(row, "col", layer, None),
        P(row, "col", layer, None, None, None),
        P(row, "col", layer, None, None),
        P(row, "col", layer),
    )
    out_specs = P(("x", "zh", "zl", "core"), "col")
    return jax.shard_map(body, mesh=split, in_specs=in_specs, out_specs=out_specs, check_vma=False)
```

```python
import jax
import jax.numpy as jnp
from jax import lax
from jax.experimental import pallas as pl
from jax.experimental.pallas import tpu as pltpu
from jax.sharding import Mesh, PartitionSpec as P

BLOCK = 64
LANES = 128
CAP_A = 8
CAP_B = 24
ROWS_A = 8
INNER = 2
COLS_B = 16
PIECES = 16
B_DATA = CAP_B // 2 * BLOCK
B_ROWS = B_DATA + 8
A_DATA = CAP_A * BLOCK
A_ROWS = A_DATA + 8
WHERE = pl.BlockSpec(memory_space=pl.ANY)
IN_VMEM = pl.BlockSpec(memory_space=pltpu.VMEM)
BIG = 56 * 1024 * 1024
FIRST = 20 * 1024 * 1024
MIDDLE = 24 * 1024 * 1024
LAST = 16 * 1024 * 1024
IN_HBM = pl.BlockSpec(memory_space=pltpu.HBM)
IN_SMEM = pl.BlockSpec(memory_space=pltpu.SMEM)


def exchange(array, axis, step):
    mask = {0: (1, 3)[step], 1: (3, 1)[step]}
    route = [(2 * i + core, 2 * (i ^ mask[core]) + core) for i in range(4) for core in range(2)]
    return lax.ppermute(array, (axis, "core"), route)


def col_partner(place, core, distance):
    if distance == 4:
        return place ^ 4
    if distance == 2:
        forward = place // 2 % 2 == (core + place) % 2
        return (place + (2 if forward else -2)) % 8
    return (place + (1 if place % 2 == core else -1)) % 8


def exchange_col(array, distance):
    route = [(2 * i + core, 2 * col_partner(i, core, distance) + core) for i in range(8) for core in range(2)]
    return lax.ppermute(array, ("col", "core"), route)


def holders(place, core):
    held = [place]
    for distance in (4, 2, 1):
        partner = holders_before(col_partner(place, core, distance), core, distance)
        held = held + partner
    return held


def holders_before(place, core, distance):
    held = [place]
    for earlier in (4, 2):
        if earlier <= distance:
            break
        held = held + holders_before(col_partner(place, core, earlier), core, earlier)
    return held


def swap(array, axis):
    return lax.ppermute(array, axis, [(0, 1), (1, 0)])


def slot_at(places, count, cols, base):
    slots = places.shape[1]
    spot = places[0:1, :] * cols + places[1:2, :] + base
    position = lax.broadcasted_iota(jnp.int32, (LANES, slots), 0)
    slot = lax.broadcasted_iota(jnp.int32, (LANES, slots), 1)
    hit = (position == spot) & (slot < count)
    return jnp.max(jnp.where(hit, slot + 1, 0), axis=1, keepdims=True)


def as_rows(column):
    return jnp.transpose(jnp.broadcast_to(column.astype(jnp.float32), (LANES, LANES)))[0:8, :]


def pack_kernel(*refs):
    ins, (a_ref, b_ref), held, sems = refs[:6], refs[6:8], refs[8:14], refs[14]
    an_ref, bn_ref, ap_ref, bp_ref, bv_ref, av_ref = held
    copies = [pltpu.make_async_copy(ins[k], held[k], sems.at[k]) for k in range(6)]
    for copy in copies:
        copy.start()
    for copy in copies[:4]:
        copy.wait()
    copy_b, copy_a = copies[4:]
    spots = slot_at(ap_ref[0], an_ref[0], INNER, 0) + slot_at(ap_ref[1], an_ref[1], INNER, 16) - 1
    a_ref[A_DATA:, :] = as_rows(spots)
    spots = slot_at(bp_ref[...], bn_ref[0, 0, 0], COLS_B, 0) - 1
    b_ref[B_DATA:, :] = as_rows(spots)
    copy_b.wait()
    for pair in range(CAP_B // 2):
        b_ref[pair * BLOCK : (pair + 1) * BLOCK, :] = jnp.concatenate(
            [bv_ref[2 * pair], bv_ref[2 * pair + 1]], axis=1
        )
    copy_a.wait()
    for pair in range(CAP_A):
        a_ref[pair * BLOCK : (pair + 1) * BLOCK, :] = jnp.concatenate(
            [av_ref[2 * pair], av_ref[2 * pair + 1]], axis=1
        )


def pack(an, bn, ap, bp, bv, av):
    return pl.pallas_call(
        pack_kernel,
        out_shape=(
            jax.ShapeDtypeStruct((A_ROWS, LANES), jnp.float32),
            jax.ShapeDtypeStruct((B_ROWS, LANES), jnp.float32),
        ),
        in_specs=[IN_HBM] * 6,
        out_specs=(IN_VMEM, IN_VMEM),
        scratch_shapes=[
            pltpu.SMEM(an.shape, jnp.int32),
            pltpu.SMEM(bn.shape, jnp.int32),
            pltpu.VMEM(ap.shape, jnp.int32),
            pltpu.VMEM(bp.shape, jnp.int32),
            pltpu.VMEM(bv.shape, jnp.float32),
            pltpu.VMEM(av.shape, jnp.float32),
            pltpu.SemaphoreType.DMA((6,)),
        ],
        compiler_params=pltpu.CompilerParams(vmem_limit_bytes=BIG),
    )(an, bn, ap, bp, bv, av)


HELD = ((0,), (4,), (1,), (8, 12), (2, 3), (5, 9, 13), (6, 10, 14), (7, 11, 15))
CALLS = ((0, 1, 12, 2, 3), (13, 14, 4, 8, 5, 9, 6, 10), (15, 7, 11))
NEAR = (0, 1, 12, 2, 3, 13, 14, 15)
LATE = CALLS[1] + CALLS[2]
FIRST_DEPTH, MIDDLE_DEPTH, LAST_DEPTH = (len(tiles) * LANES for tiles in CALLS)


def block_pair(load, left, right):
    lane = lax.broadcasted_iota(jnp.int32, (BLOCK, LANES), 1)
    low = jnp.maximum(left, 0)
    high = jnp.maximum(right, 0)
    one = pltpu.roll(load(low // 2), (low % 2) * BLOCK, 1)
    two = pltpu.roll(load(high // 2), (1 - high % 2) * BLOCK, 1)
    one = jnp.where((lane < BLOCK) & (left >= 0), one, 0.0)
    return jnp.where((lane >= BLOCK) & (right >= 0), two, one)


def halves(value):
    top = value.astype(jnp.bfloat16)
    return top, (value - top.astype(jnp.float32)).astype(jnp.bfloat16)


def ring_place(mask, core):
    near = jnp.where(mask == 1 + 2 * core, 1, 2)
    return jnp.where(mask == 0, 0, jnp.where(mask == 2, 3, near))


def place_left(me_ref, first, a_f, spots_s, a_hi, a_lo):
    x, zh, col, zl, core = (me_ref[k] for k in range(5))

    def left_tile(index, _):
        source = index // 2
        slot = index % 2
        holder = me_ref[5 + PIECES + (2 * col + core) * 8 + first + source]
        owner = (4 * x + zh + holder + 8 * slot + PIECES - col) % PIECES
        dx = ring_place((owner // 4) ^ x, core)
        dz = ring_place((owner % 4) ^ zh, core)
        at = me_ref[5 + 4 * dz + dx]
        lanes = pl.ds(pl.multiple_of(at * LANES, LANES), LANES)
        for r in range(ROWS_A):
            quarter = r // 2
            place = jnp.where(quarter % 2 == core, 2, 0) + jnp.where(quarter // 2 == zl, 1, 0)
            rows = pl.ds(pl.multiple_of(place * 128 + (r % 2) * BLOCK, BLOCK), BLOCK)

            def load(pair):
                return a_f[source, pl.ds(pl.multiple_of((slot * 4 + pair) * BLOCK, BLOCK), BLOCK), :]

            left = spots_s[source, slot * 16 + 2 * r].astype(jnp.int32)
            right = spots_s[source, slot * 16 + 2 * r + 1].astype(jnp.int32)
            a_hi[rows, lanes], a_lo[rows, lanes] = halves(block_pair(load, left, right))
        return 0

    lax.fori_loop(0, 8, left_tile, 0)


def right_copies(call, b_in, b_f, spots_s, sem_b, sem_s):
    tiles = CALLS[call]
    copies, spots = [], []
    for source, held in zip(b_in, [held for held in HELD if set(held) & set(tiles)], strict=True):
        for k, tile in enumerate(held):
            if tile not in tiles:
                continue
            at = tiles.index(tile)
            rows = pl.ds(k * B_ROWS, B_ROWS)
            copies.append(pltpu.make_async_copy(source.at[rows], b_f.at[at], sem_b.at[at]))
            spots.append(pltpu.make_async_copy(source.at[k * B_ROWS + B_DATA], spots_s.at[at], sem_s.at[at]))
    return copies, spots


def place_right(tiles, b_f, spots_s, b_hi, b_lo):
    def right_tile(tile, _):
        for k in range(INNER):
            rows = pl.ds(pl.multiple_of(tile * LANES + k * BLOCK, BLOCK), BLOCK)
            for c in range(COLS_B // 2):

                def load(pair):
                    return b_f[tile, pl.ds(pl.multiple_of(pair * BLOCK, BLOCK), BLOCK), :]

                spot = k * COLS_B + 2 * c
                left = spots_s[tile, spot].astype(jnp.int32)
                right = spots_s[tile, spot + 1].astype(jnp.int32)
                lanes = slice(c * LANES, (c + 1) * LANES)
                b_hi[rows, lanes], b_lo[rows, lanes] = halves(block_pair(load, left, right))
        return 0

    lax.fori_loop(0, tiles, right_tile, 0)


def left_copies(parts, a_f, spots_s, sem_a, sem_s):
    copies, spots = [], []
    for n, (part, k) in enumerate([(part, k) for part in parts for k in range(part.shape[0] // A_ROWS)]):
        copies.append(pltpu.make_async_copy(part.at[pl.ds(k * A_ROWS, A_ROWS)], a_f.at[n], sem_a.at[n]))
        spots.append(pltpu.make_async_copy(part.at[k * A_ROWS + A_DATA], spots_s.at[n], sem_s.at[n]))
    return copies, spots


def partial_product(left_hi, left_lo, b_hi, b_lo, store):
    for n in range(4):
        lanes = slice(n * 256, (n + 1) * 256)
        top = b_hi[:, lanes]
        total = jnp.dot(left_lo, top, preferred_element_type=jnp.float32)
        total += jnp.dot(left_hi, b_lo[:, lanes], preferred_element_type=jnp.float32)
        total += jnp.dot(left_hi, top, preferred_element_type=jnp.float32)
        store(lanes, total)


def early_kernel(n_right, *refs):
    b_in = refs[:n_right]
    b_hi, b_lo, b_f, spots_b, sem_b, sem_s = refs[n_right:]
    copies, spots = right_copies(0, b_in, b_f, spots_b, sem_b, sem_s)
    for copy in spots + copies:
        copy.start()
    for copy in spots + copies:
        copy.wait()
    place_right(len(CALLS[0]), b_f, spots_b, b_hi, b_lo)


def first_kernel(*refs):
    me_ref, a_in, b_in = refs[0], refs[1:4], refs[4:6]
    near_hi, near_lo, c_out = refs[6:9]
    a_f, spots_a, sem_a, sem_sa, b_hi, b_lo, sem_b = refs[9:]
    copies_a, spots_of_a = left_copies(a_in, a_f, spots_a, sem_a, sem_sa)
    copies = [pltpu.make_async_copy(b_in[k], (b_hi, b_lo)[k], sem_b.at[k]) for k in range(2)]
    for copy in spots_of_a + copies_a + copies:
        copy.start()
    for copy in spots_of_a + copies_a:
        copy.wait()
    place_left(me_ref, 0, a_f, spots_a, near_hi, near_lo)
    for copy in copies:
        copy.wait()

    def store(lanes, total):
        c_out[:, lanes] = total

    partial_product(near_hi[:, :FIRST_DEPTH], near_lo[:, :FIRST_DEPTH], b_hi, b_lo, store)


def middle_kernel(n_right, *refs):
    me_ref, a_in, near, c_in, b_in = refs[0], refs[1], refs[2:4], refs[4], refs[5 : 5 + n_right]
    late_hi, late_lo, c_out = refs[5 + n_right : 8 + n_right]
    a_f, spots_a, sem_a, sem_sa, c_held, sem_c, b_f, b_hi, b_lo, spots_b, sem_b, sem_s = refs[8 + n_right :]
    copies_a, spots_of_a = left_copies((a_in,), a_f, spots_a, sem_a, sem_sa)
    copies, spots = right_copies(1, b_in, b_f, spots_b, sem_b, sem_s)
    held = [pltpu.make_async_copy(c_in, c_held, sem_c.at[0])]
    for k, late in enumerate((late_hi, late_lo)):
        for n, (first, at, lanes) in enumerate(((FIRST_DEPTH, 0, 256), (FIRST_DEPTH + 256, MIDDLE_DEPTH, 128))):
            source = near[k].at[:, pl.ds(first, lanes)]
            held.append(pltpu.make_async_copy(source, late.at[:, pl.ds(at, lanes)], sem_c.at[1 + 2 * k + n]))
    for copy in spots_of_a + copies_a + spots + copies + held:
        copy.start()
    for copy in spots_of_a + copies_a:
        copy.wait()
    place_left(me_ref, 4, a_f, spots_a, late_hi, late_lo)
    for copy in spots + copies:
        copy.wait()
    place_right(len(CALLS[1]), b_f, spots_b, b_hi, b_lo)
    for copy in held:
        copy.wait()

    def store(lanes, total):
        c_out[:, lanes] = total + c_held[:, lanes]

    partial_product(late_hi[:, :MIDDLE_DEPTH], late_lo[:, :MIDDLE_DEPTH], b_hi, b_lo, store)


def last_kernel(n_right, *refs):
    late_hi, late_lo, c_in = refs[:3]
    b_in = refs[3 : 3 + n_right]
    other, send, keep, b_f, b_hi, b_lo, spots_b, sem_b, sem_s = refs[3 + n_right :]
    copies, spots = right_copies(2, b_in, b_f, spots_b, sem_b, sem_s)
    for copy in spots + copies:
        copy.start()
    for copy in spots + copies:
        copy.wait()
    place_right(len(CALLS[2]), b_f, spots_b, b_hi, b_lo)

    def store(lanes, total):
        total += c_in[:, lanes]
        other[:, lanes] = total[:256]
        send[:, lanes] = total[256:384]
        keep[:, lanes] = total[384:]

    partial_product(late_hi[:, MIDDLE_DEPTH:], late_lo[:, MIDDLE_DEPTH:], b_hi, b_lo, store)


def right_scratch(call):
    tiles = len(CALLS[call])
    return [
        pltpu.VMEM((tiles, B_ROWS, LANES), jnp.float32),
        pltpu.VMEM((tiles * LANES, 1024), jnp.bfloat16),
        pltpu.VMEM((tiles * LANES, 1024), jnp.bfloat16),
        pltpu.SMEM((tiles, LANES), jnp.float32),
        pltpu.SemaphoreType.DMA((tiles,)),
        pltpu.SemaphoreType.DMA((tiles,)),
    ]


def used_by(call, b_all):
    return [b_all[k] for k in range(len(HELD)) if set(HELD[k]) & set(CALLS[call])]


def cost(call):
    flops = 3 * 2 * 512 * 1024 * LANES * len(CALLS[call])
    return pl.CostEstimate(flops=flops, bytes_accessed=16 * 1024 * 1024, transcendentals=0)


LEFT_SCRATCH = (
    pltpu.VMEM((4, A_ROWS, LANES), jnp.float32),
    pltpu.SMEM((4, LANES), jnp.float32),
    pltpu.SemaphoreType.DMA((4,)),
    pltpu.SemaphoreType.DMA((4,)),
)


def early_right(b_all):
    operands = used_by(0, b_all)
    dense = jax.ShapeDtypeStruct((FIRST_DEPTH, 1024), jnp.bfloat16)
    scratch = right_scratch(0)
    return pl.pallas_call(
        lambda *refs: early_kernel(len(operands), *refs),
        out_shape=(dense, dense),
        in_specs=[WHERE] * len(operands),
        out_specs=(IN_VMEM,) * 2,
        scratch_shapes=scratch[:1] + scratch[3:],
        compiler_params=pltpu.CompilerParams(vmem_limit_bytes=FIRST),
        cost_estimate=pl.CostEstimate(flops=10**9, bytes_accessed=16 * 1024 * 1024, transcendentals=0),
    )(*operands)


def first_product(me, a_near, right):
    near = jax.ShapeDtypeStruct((512, len(NEAR) * LANES), jnp.bfloat16)
    return pl.pallas_call(
        first_kernel,
        out_shape=(near, near, jax.ShapeDtypeStruct((512, 1024), jnp.float32)),
        in_specs=[IN_SMEM] + [WHERE] * 5,
        out_specs=(IN_VMEM,) * 3,
        scratch_shapes=[*LEFT_SCRATCH, *right_scratch(0)[1:3], pltpu.SemaphoreType.DMA((2,))],
        compiler_params=pltpu.CompilerParams(vmem_limit_bytes=FIRST),
        cost_estimate=cost(0),
    )(me, *a_near, *right)


def middle_product(me, a_far, near_hi, near_lo, so_far, b_all):
    operands = used_by(1, b_all)
    late = jax.ShapeDtypeStruct((512, len(LATE) * LANES), jnp.bfloat16)
    return pl.pallas_call(
        lambda *refs: middle_kernel(len(operands), *refs),
        out_shape=(late, late, jax.ShapeDtypeStruct((512, 1024), jnp.float32)),
        in_specs=[IN_SMEM] + [WHERE] * (4 + len(operands)),
        out_specs=(IN_VMEM,) * 3,
        scratch_shapes=[
            *LEFT_SCRATCH,
            pltpu.VMEM((512, 1024), jnp.float32),
            pltpu.SemaphoreType.DMA((5,)),
            *right_scratch(1),
        ],
        compiler_params=pltpu.CompilerParams(vmem_limit_bytes=MIDDLE),
        cost_estimate=cost(1),
    )(me, a_far, near_hi, near_lo, so_far, *operands)


def last_product(late_hi, late_lo, so_far, b_all):
    operands = used_by(2, b_all)
    return pl.pallas_call(
        lambda *refs: last_kernel(len(operands), *refs),
        out_shape=tuple(jax.ShapeDtypeStruct((rows, 1024), jnp.float32) for rows in (256, 128, 128)),
        in_specs=[IN_VMEM] * 3 + [WHERE] * len(operands),
        out_specs=(IN_VMEM,) * 3,
        scratch_shapes=right_scratch(2),
        compiler_params=pltpu.CompilerParams(vmem_limit_bytes=LAST),
        cost_estimate=cost(2),
    )(late_hi, late_lo, so_far, *operands)


def body(a_values, a_places, a_counts, b_values, b_places, b_counts):
    hold = lax.optimization_barrier
    by_place = [holder for place in range(8) for core in range(2) for holder in holders(place, core)]
    me = [lax.axis_index(name) for name in ("x", "zh", "col", "zl", "core")]
    table = jnp.array([(NEAR if tile in NEAR else LATE).index(tile) for tile in range(PIECES)] + by_place, jnp.int32)
    me = jnp.concatenate([jnp.stack(me).astype(jnp.int32), table])
    own_a, own = pack(
        a_counts.reshape(2),
        b_counts,
        a_places.reshape(2, CAP_A, 2).swapaxes(1, 2),
        b_places.reshape(CAP_B, 2).swapaxes(0, 1),
        b_values.reshape(CAP_B, BLOCK, BLOCK),
        a_values.reshape(2 * CAP_A, BLOCK, BLOCK),
    )
    z_one = exchange(own, "zh", 0)
    x_one = exchange(own, "x", 0)
    x_one, z_one, own_a = hold((x_one, z_one, own_a))
    a_one = exchange_col(own_a, 4)

    z_two = exchange(jnp.concatenate([own, z_one], axis=0), "zh", 1)
    x_two = exchange(jnp.concatenate([own, x_one], axis=0), "x", 1)
    x_two, z_two = hold((x_two, z_two))
    a_one, _ = hold((a_one, z_two))
    a_two = exchange_col(jnp.concatenate([own_a, a_one], axis=0), 2)

    column = jnp.concatenate([z_one, z_two], axis=0)
    x_three = exchange(column, "x", 0)
    x_four = exchange(column, "x", 1)
    b_all = [own, z_one, x_one, z_two, x_two]
    right = early_right(b_all)
    a_two, *right = hold((a_two, *right))
    a_four = exchange_col(jnp.concatenate([own_a, a_one, a_two], axis=0), 1)
    x_three, a_two = hold((x_three, a_two))
    near_hi, near_lo, total = first_product(me, (own_a, a_one, a_two), right)
    b_all += [x_three, x_four, exchange(x_three, "x", 1)]
    late_hi, late_lo, total = middle_product(me, a_four, near_hi, near_lo, total, b_all)
    other, send, keep = last_product(late_hi, late_lo, total, b_all)

    got = swap(other, "core")
    ahead = swap(send + got[:128], "zl")
    return (keep + got[128:]) + ahead


def solution(mesh):
    split = Mesh(mesh.devices.reshape(4, 4, 8, 2, 2), ("x", "zh", "col", "zl", "core"))
    row, layer = ("x", "zh"), ("zl", "core")
    in_specs = (
        P(row, "col", layer, None, None, None, None),
        P(row, "col", layer, None, None, None),
        P(row, "col", layer, None),
        P(row, "col", layer, None, None, None),
        P(row, "col", layer, None, None),
        P(row, "col", layer),
    )
    out_specs = P(("x", "zh", "zl", "core"), "col")
    return jax.shard_map(body, mesh=split, in_specs=in_specs, out_specs=out_specs, check_vma=False)
```

```python
import jax
import jax.numpy as jnp
from jax import lax
from jax.experimental import pallas as pl
from jax.experimental.pallas import tpu as pltpu
from jax.sharding import Mesh, PartitionSpec as P

BLOCK = 64
LANES = 128
CAP_A = 8
CAP_B = 24
ROWS_A = 8
INNER = 2
COLS_B = 16
PIECES = 16
B_DATA = CAP_B // 2 * BLOCK
B_ROWS = B_DATA + 8
A_DATA = CAP_A * BLOCK
A_ROWS = A_DATA + 8
WHERE = pl.BlockSpec(memory_space=pl.ANY)
IN_VMEM = pl.BlockSpec(memory_space=pltpu.VMEM)
BIG = 56 * 1024 * 1024
FIRST = 20 * 1024 * 1024
MIDDLE = 24 * 1024 * 1024
LAST = 16 * 1024 * 1024
IN_HBM = pl.BlockSpec(memory_space=pltpu.HBM)
IN_SMEM = pl.BlockSpec(memory_space=pltpu.SMEM)


def exchange(array, axis, step):
    mask = {0: (1, 3)[step], 1: (3, 1)[step]}
    route = [(2 * i + core, 2 * (i ^ mask[core]) + core) for i in range(4) for core in range(2)]
    return lax.ppermute(array, (axis, "core"), route)


def col_partner(place, core, distance):
    if distance == 4:
        return place ^ 4
    if distance == 2:
        forward = place // 2 % 2 == (core + place) % 2
        return (place + (2 if forward else -2)) % 8
    return (place + (1 if place % 2 == core else -1)) % 8


def exchange_col(array, distance):
    route = [(2 * i + core, 2 * col_partner(i, core, distance) + core) for i in range(8) for core in range(2)]
    return lax.ppermute(array, ("col", "core"), route)


def holders(place, core):
    held = [place]
    for distance in (4, 2, 1):
        partner = holders_before(col_partner(place, core, distance), core, distance)
        held = held + partner
    return held


def holders_before(place, core, distance):
    held = [place]
    for earlier in (4, 2):
        if earlier <= distance:
            break
        held = held + holders_before(col_partner(place, core, earlier), core, earlier)
    return held


def swap(array, axis):
    return lax.ppermute(array, axis, [(0, 1), (1, 0)])


def slot_at(places, count, cols, base):
    slots = places.shape[1]
    spot = places[0:1, :] * cols + places[1:2, :] + base
    position = lax.broadcasted_iota(jnp.int32, (LANES, slots), 0)
    slot = lax.broadcasted_iota(jnp.int32, (LANES, slots), 1)
    hit = (position == spot) & (slot < count)
    return jnp.max(jnp.where(hit, slot + 1, 0), axis=1, keepdims=True)


def as_rows(column):
    return jnp.transpose(jnp.broadcast_to(column.astype(jnp.float32), (LANES, LANES)))[0:8, :]


def pack_kernel(*refs):
    ins, (a_ref, b_ref), held, sems = refs[:6], refs[6:8], refs[8:14], refs[14]
    an_ref, bn_ref, ap_ref, bp_ref, bv_ref, av_ref = held
    copies = [pltpu.make_async_copy(ins[k], held[k], sems.at[k]) for k in range(6)]
    for copy in copies:
        copy.start()
    for copy in copies[:4]:
        copy.wait()
    copy_b, copy_a = copies[4:]
    spots = slot_at(ap_ref[0], an_ref[0], INNER, 0) + slot_at(ap_ref[1], an_ref[1], INNER, 16) - 1
    a_ref[A_DATA:, :] = as_rows(spots)
    spots = slot_at(bp_ref[...], bn_ref[0, 0, 0], COLS_B, 0) - 1
    b_ref[B_DATA:, :] = as_rows(spots)
    copy_b.wait()
    for pair in range(CAP_B // 2):
        b_ref[pair * BLOCK : (pair + 1) * BLOCK, :] = jnp.concatenate(
            [bv_ref[2 * pair], bv_ref[2 * pair + 1]], axis=1
        )
    copy_a.wait()
    for pair in range(CAP_A):
        a_ref[pair * BLOCK : (pair + 1) * BLOCK, :] = jnp.concatenate(
            [av_ref[2 * pair], av_ref[2 * pair + 1]], axis=1
        )


def pack(an, bn, ap, bp, bv, av):
    return pl.pallas_call(
        pack_kernel,
        out_shape=(
            jax.ShapeDtypeStruct((A_ROWS, LANES), jnp.float32),
            jax.ShapeDtypeStruct((B_ROWS, LANES), jnp.float32),
        ),
        in_specs=[IN_HBM] * 6,
        out_specs=(IN_VMEM, IN_VMEM),
        scratch_shapes=[
            pltpu.SMEM(an.shape, jnp.int32),
            pltpu.SMEM(bn.shape, jnp.int32),
            pltpu.VMEM(ap.shape, jnp.int32),
            pltpu.VMEM(bp.shape, jnp.int32),
            pltpu.VMEM(bv.shape, jnp.float32),
            pltpu.VMEM(av.shape, jnp.float32),
            pltpu.SemaphoreType.DMA((6,)),
        ],
        compiler_params=pltpu.CompilerParams(vmem_limit_bytes=BIG),
    )(an, bn, ap, bp, bv, av)


HELD = ((0,), (4,), (1,), (8, 12), (2, 3), (5, 9, 13), (6, 10, 14), (7, 11, 15))
CALLS = ((0, 1, 12, 2, 3), (4, 8, 13, 14, 5, 9, 6, 10), (15, 7, 11))
PLACED = ((0, 1, 12, 2, 3, 4, 8), (13, 14, 5, 9, 6, 10), (15, 7, 11))
AHEAD = 2 * LANES
NEAR = (0, 1, 12, 2, 3, 13, 14, 15)
LATE = CALLS[1] + CALLS[2]
FIRST_DEPTH, MIDDLE_DEPTH, LAST_DEPTH = (len(tiles) * LANES for tiles in CALLS)


def block_pair(load, left, right):
    lane = lax.broadcasted_iota(jnp.int32, (BLOCK, LANES), 1)
    low = jnp.maximum(left, 0)
    high = jnp.maximum(right, 0)
    one = pltpu.roll(load(low // 2), (low % 2) * BLOCK, 1)
    two = pltpu.roll(load(high // 2), (1 - high % 2) * BLOCK, 1)
    one = jnp.where((lane < BLOCK) & (left >= 0), one, 0.0)
    return jnp.where((lane >= BLOCK) & (right >= 0), two, one)


def halves(value):
    top = value.astype(jnp.bfloat16)
    return top, (value - top.astype(jnp.float32)).astype(jnp.bfloat16)


def ring_place(mask, core):
    near = jnp.where(mask == 1 + 2 * core, 1, 2)
    return jnp.where(mask == 0, 0, jnp.where(mask == 2, 3, near))


def place_left(me_ref, first, a_f, spots_s, a_hi, a_lo):
    x, zh, col, zl, core = (me_ref[k] for k in range(5))

    def left_tile(index, _):
        source = index // 2
        slot = index % 2
        holder = me_ref[5 + PIECES + (2 * col + core) * 8 + first + source]
        owner = (4 * x + zh + holder + 8 * slot + PIECES - col) % PIECES
        dx = ring_place((owner // 4) ^ x, core)
        dz = ring_place((owner % 4) ^ zh, core)
        at = me_ref[5 + 4 * dz + dx]
        lanes = pl.ds(pl.multiple_of(at * LANES, LANES), LANES)
        for r in range(ROWS_A):
            quarter = r // 2
            place = jnp.where(quarter % 2 == core, 2, 0) + jnp.where(quarter // 2 == zl, 1, 0)
            rows = pl.ds(pl.multiple_of(place * 128 + (r % 2) * BLOCK, BLOCK), BLOCK)

            def load(pair):
                return a_f[source, pl.ds(pl.multiple_of((slot * 4 + pair) * BLOCK, BLOCK), BLOCK), :]

            left = spots_s[source, slot * 16 + 2 * r].astype(jnp.int32)
            right = spots_s[source, slot * 16 + 2 * r + 1].astype(jnp.int32)
            a_hi[rows, lanes], a_lo[rows, lanes] = halves(block_pair(load, left, right))
        return 0

    lax.fori_loop(0, 8, left_tile, 0)


def right_copies(call, b_in, b_f, spots_s, sem_b, sem_s):
    tiles = PLACED[call]
    copies, spots = [], []
    for source, held in zip(b_in, [held for held in HELD if set(held) & set(tiles)], strict=True):
        for k, tile in enumerate(held):
            if tile not in tiles:
                continue
            at = tiles.index(tile)
            rows = pl.ds(k * B_ROWS, B_ROWS)
            copies.append(pltpu.make_async_copy(source.at[rows], b_f.at[at], sem_b.at[at]))
            spots.append(pltpu.make_async_copy(source.at[k * B_ROWS + B_DATA], spots_s.at[at], sem_s.at[at]))
    return copies, spots


def place_right(first, tiles, b_f, spots_s, b_hi, b_lo):
    def right_tile(tile, _):
        for k in range(INNER):
            rows = pl.ds(pl.multiple_of(tile * LANES + k * BLOCK, BLOCK), BLOCK)
            for c in range(COLS_B // 2):

                def load(pair):
                    return b_f[first + tile, pl.ds(pl.multiple_of(pair * BLOCK, BLOCK), BLOCK), :]

                spot = k * COLS_B + 2 * c
                left = spots_s[first + tile, spot].astype(jnp.int32)
                right = spots_s[first + tile, spot + 1].astype(jnp.int32)
                lanes = slice(c * LANES, (c + 1) * LANES)
                b_hi[rows, lanes], b_lo[rows, lanes] = halves(block_pair(load, left, right))
        return 0

    lax.fori_loop(0, tiles, right_tile, 0)


def left_copies(parts, a_f, spots_s, sem_a, sem_s):
    copies, spots = [], []
    for n, (part, k) in enumerate([(part, k) for part in parts for k in range(part.shape[0] // A_ROWS)]):
        copies.append(pltpu.make_async_copy(part.at[pl.ds(k * A_ROWS, A_ROWS)], a_f.at[n], sem_a.at[n]))
        spots.append(pltpu.make_async_copy(part.at[k * A_ROWS + A_DATA], spots_s.at[n], sem_s.at[n]))
    return copies, spots


def partial_product(left_hi, left_lo, b_hi, b_lo, store):
    for n in range(4):
        lanes = slice(n * 256, (n + 1) * 256)
        top = b_hi[:, lanes]
        total = jnp.dot(left_lo, top, preferred_element_type=jnp.float32)
        total += jnp.dot(left_hi, b_lo[:, lanes], preferred_element_type=jnp.float32)
        total += jnp.dot(left_hi, top, preferred_element_type=jnp.float32)
        store(lanes, total)


def early_kernel(n_right, *refs):
    b_in = refs[:n_right]
    b_hi, b_lo, ahead_hi, ahead_lo, b_f, spots_b, sem_b, sem_s = refs[n_right:]
    copies, spots = right_copies(0, b_in, b_f, spots_b, sem_b, sem_s)
    for copy in spots + copies:
        copy.start()
    for copy in spots + copies:
        copy.wait()
    place_right(0, len(CALLS[0]), b_f, spots_b, b_hi, b_lo)
    place_right(len(CALLS[0]), 2, b_f, spots_b, ahead_hi, ahead_lo)


def first_kernel(*refs):
    me_ref, a_in, b_in = refs[0], refs[1:4], refs[4:6]
    near_hi, near_lo, c_out = refs[6:9]
    a_f, spots_a, sem_a, sem_sa, b_hi, b_lo, sem_b = refs[9:]
    copies_a, spots_of_a = left_copies(a_in, a_f, spots_a, sem_a, sem_sa)
    copies = [pltpu.make_async_copy(b_in[k], (b_hi, b_lo)[k], sem_b.at[k]) for k in range(2)]
    for copy in spots_of_a + copies_a + copies:
        copy.start()
    for copy in spots_of_a + copies_a:
        copy.wait()
    place_left(me_ref, 0, a_f, spots_a, near_hi, near_lo)
    for copy in copies:
        copy.wait()

    def store(lanes, total):
        c_out[:, lanes] = total

    partial_product(near_hi[:, :FIRST_DEPTH], near_lo[:, :FIRST_DEPTH], b_hi, b_lo, store)


def middle_kernel(n_right, *refs):
    me_ref, a_in, near, c_in, ahead, b_in = refs[0], refs[1], refs[2:4], refs[4], refs[5:7], refs[7 : 7 + n_right]
    late_hi, late_lo, c_out = refs[7 + n_right : 10 + n_right]
    a_f, spots_a, sem_a, sem_sa, c_held, sem_c, b_f, b_hi, b_lo, spots_b, sem_b, sem_s = refs[10 + n_right :]
    copies_a, spots_of_a = left_copies((a_in,), a_f, spots_a, sem_a, sem_sa)
    copies, spots = right_copies(1, b_in, b_f, spots_b, sem_b, sem_s)
    held = [pltpu.make_async_copy(c_in, c_held, sem_c.at[0])]
    for k, dense in enumerate((b_hi, b_lo)):
        held.append(pltpu.make_async_copy(ahead[k], dense.at[pl.ds(0, AHEAD)], sem_c.at[5 + k]))
    for k, late in enumerate((late_hi, late_lo)):
        for n, (first, at, lanes) in enumerate(((FIRST_DEPTH, AHEAD, 256), (FIRST_DEPTH + 256, MIDDLE_DEPTH, 128))):
            source = near[k].at[:, pl.ds(first, lanes)]
            held.append(pltpu.make_async_copy(source, late.at[:, pl.ds(at, lanes)], sem_c.at[1 + 2 * k + n]))
    for copy in spots_of_a + copies_a + spots + copies + held:
        copy.start()
    for copy in spots_of_a + copies_a:
        copy.wait()
    place_left(me_ref, 4, a_f, spots_a, late_hi, late_lo)
    for copy in spots + copies:
        copy.wait()
    rest = pl.ds(AHEAD, MIDDLE_DEPTH - AHEAD)
    place_right(0, len(PLACED[1]), b_f, spots_b, b_hi.at[rest], b_lo.at[rest])
    for copy in held:
        copy.wait()

    def store(lanes, total):
        c_out[:, lanes] = total + c_held[:, lanes]

    partial_product(late_hi[:, :MIDDLE_DEPTH], late_lo[:, :MIDDLE_DEPTH], b_hi, b_lo, store)


def last_kernel(n_right, *refs):
    late_hi, late_lo, c_in = refs[:3]
    b_in = refs[3 : 3 + n_right]
    other, send, keep, b_f, b_hi, b_lo, spots_b, sem_b, sem_s = refs[3 + n_right :]
    copies, spots = right_copies(2, b_in, b_f, spots_b, sem_b, sem_s)
    for copy in spots + copies:
        copy.start()
    for copy in spots + copies:
        copy.wait()
    place_right(0, len(CALLS[2]), b_f, spots_b, b_hi, b_lo)

    def store(lanes, total):
        total += c_in[:, lanes]
        other[:, lanes] = total[:256]
        send[:, lanes] = total[256:384]
        keep[:, lanes] = total[384:]

    partial_product(late_hi[:, MIDDLE_DEPTH:], late_lo[:, MIDDLE_DEPTH:], b_hi, b_lo, store)


def right_scratch(call):
    tiles, depth = len(PLACED[call]), len(CALLS[call]) * LANES
    return [
        pltpu.VMEM((tiles, B_ROWS, LANES), jnp.float32),
        pltpu.VMEM((depth, 1024), jnp.bfloat16),
        pltpu.VMEM((depth, 1024), jnp.bfloat16),
        pltpu.SMEM((tiles, LANES), jnp.float32),
        pltpu.SemaphoreType.DMA((tiles,)),
        pltpu.SemaphoreType.DMA((tiles,)),
    ]


def used_by(call, b_all):
    return [b_all[k] for k in range(len(HELD)) if set(HELD[k]) & set(PLACED[call])]


def cost(call):
    flops = 3 * 2 * 512 * 1024 * LANES * len(CALLS[call])
    return pl.CostEstimate(flops=flops, bytes_accessed=16 * 1024 * 1024, transcendentals=0)


LEFT_SCRATCH = (
    pltpu.VMEM((4, A_ROWS, LANES), jnp.float32),
    pltpu.SMEM((4, LANES), jnp.float32),
    pltpu.SemaphoreType.DMA((4,)),
    pltpu.SemaphoreType.DMA((4,)),
)


def early_right(b_all):
    operands = used_by(0, b_all)
    dense = jax.ShapeDtypeStruct((FIRST_DEPTH, 1024), jnp.bfloat16)
    ahead = jax.ShapeDtypeStruct((AHEAD, 1024), jnp.bfloat16)
    scratch = right_scratch(0)
    return pl.pallas_call(
        lambda *refs: early_kernel(len(operands), *refs),
        out_shape=(dense, dense, ahead, ahead),
        in_specs=[WHERE] * len(operands),
        out_specs=(IN_VMEM,) * 4,
        scratch_shapes=scratch[:1] + scratch[3:],
        compiler_params=pltpu.CompilerParams(vmem_limit_bytes=FIRST),
        cost_estimate=pl.CostEstimate(flops=10**9, bytes_accessed=16 * 1024 * 1024, transcendentals=0),
    )(*operands)


def first_product(me, a_near, right):
    near = jax.ShapeDtypeStruct((512, len(NEAR) * LANES), jnp.bfloat16)
    return pl.pallas_call(
        first_kernel,
        out_shape=(near, near, jax.ShapeDtypeStruct((512, 1024), jnp.float32)),
        in_specs=[IN_SMEM] + [WHERE] * 5,
        out_specs=(IN_VMEM,) * 3,
        scratch_shapes=[*LEFT_SCRATCH, *right_scratch(0)[1:3], pltpu.SemaphoreType.DMA((2,))],
        compiler_params=pltpu.CompilerParams(vmem_limit_bytes=FIRST),
        cost_estimate=cost(0),
    )(me, *a_near, *right)


def middle_product(me, a_far, near_hi, near_lo, so_far, ahead, b_all):
    operands = used_by(1, b_all)
    late = jax.ShapeDtypeStruct((512, len(LATE) * LANES), jnp.bfloat16)
    return pl.pallas_call(
        lambda *refs: middle_kernel(len(operands), *refs),
        out_shape=(late, late, jax.ShapeDtypeStruct((512, 1024), jnp.float32)),
        in_specs=[IN_SMEM] + [WHERE] * (6 + len(operands)),
        out_specs=(IN_VMEM,) * 3,
        scratch_shapes=[
            *LEFT_SCRATCH,
            pltpu.VMEM((512, 1024), jnp.float32),
            pltpu.SemaphoreType.DMA((7,)),
            *right_scratch(1),
        ],
        compiler_params=pltpu.CompilerParams(vmem_limit_bytes=MIDDLE),
        cost_estimate=cost(1),
    )(me, a_far, near_hi, near_lo, so_far, *ahead, *operands)


def last_product(late_hi, late_lo, so_far, b_all):
    operands = used_by(2, b_all)
    return pl.pallas_call(
        lambda *refs: last_kernel(len(operands), *refs),
        out_shape=tuple(jax.ShapeDtypeStruct((rows, 1024), jnp.float32) for rows in (256, 128, 128)),
        in_specs=[IN_VMEM] * 3 + [WHERE] * len(operands),
        out_specs=(IN_VMEM,) * 3,
        scratch_shapes=right_scratch(2),
        compiler_params=pltpu.CompilerParams(vmem_limit_bytes=LAST),
        cost_estimate=cost(2),
    )(late_hi, late_lo, so_far, *operands)


def body(a_values, a_places, a_counts, b_values, b_places, b_counts):
    hold = lax.optimization_barrier
    by_place = [holder for place in range(8) for core in range(2) for holder in holders(place, core)]
    me = [lax.axis_index(name) for name in ("x", "zh", "col", "zl", "core")]
    table = jnp.array([(NEAR if tile in NEAR else LATE).index(tile) for tile in range(PIECES)] + by_place, jnp.int32)
    me = jnp.concatenate([jnp.stack(me).astype(jnp.int32), table])
    own_a, own = pack(
        a_counts.reshape(2),
        b_counts,
        a_places.reshape(2, CAP_A, 2).swapaxes(1, 2),
        b_places.reshape(CAP_B, 2).swapaxes(0, 1),
        b_values.reshape(CAP_B, BLOCK, BLOCK),
        a_values.reshape(2 * CAP_A, BLOCK, BLOCK),
    )
    z_one = exchange(own, "zh", 0)
    x_one = exchange(own, "x", 0)
    x_one, z_one, own_a = hold((x_one, z_one, own_a))
    a_one = exchange_col(own_a, 4)

    z_two = exchange(jnp.concatenate([own, z_one], axis=0), "zh", 1)
    x_two = exchange(jnp.concatenate([own, x_one], axis=0), "x", 1)
    x_two, z_two = hold((x_two, z_two))
    a_one, _ = hold((a_one, z_two))
    a_two = exchange_col(jnp.concatenate([own_a, a_one], axis=0), 2)

    column = jnp.concatenate([z_one, z_two], axis=0)
    x_three = exchange(column, "x", 0)
    x_four = exchange(column, "x", 1)
    b_all = [own, z_one, x_one, z_two, x_two]
    right = early_right(b_all)
    a_two, *right = hold((a_two, *right))
    a_four = exchange_col(jnp.concatenate([own_a, a_one, a_two], axis=0), 1)
    x_three, a_two = hold((x_three, a_two))
    near_hi, near_lo, total = first_product(me, (own_a, a_one, a_two), right[:2])
    b_all += [x_three, x_four, exchange(x_three, "x", 1)]
    late_hi, late_lo, total = middle_product(me, a_four, near_hi, near_lo, total, right[2:], b_all)
    other, send, keep = last_product(late_hi, late_lo, total, b_all)

    got = swap(other, "core")
    ahead = swap(send + got[:128], "zl")
    return (keep + got[128:]) + ahead


def solution(mesh):
    split = Mesh(mesh.devices.reshape(4, 4, 8, 2, 2), ("x", "zh", "col", "zl", "core"))
    row, layer = ("x", "zh"), ("zl", "core")
    in_specs = (
        P(row, "col", layer, None, None, None, None),
        P(row, "col", layer, None, None, None),
        P(row, "col", layer, None),
        P(row, "col", layer, None, None, None),
        P(row, "col", layer, None, None),
        P(row, "col", layer),
    )
    out_specs = P(("x", "zh", "zl", "core"), "col")
    return jax.shard_map(body, mesh=split, in_specs=in_specs, out_specs=out_specs, check_vma=False)
```

```python
import jax
import jax.numpy as jnp
from jax import lax
from jax.experimental import pallas as pl
from jax.experimental.pallas import tpu as pltpu
from jax.sharding import Mesh, PartitionSpec as P

BLOCK = 64
LANES = 128
CAP_A = 8
CAP_B = 24
ROWS_A = 8
INNER = 2
COLS_B = 16
PIECES = 16
B_DATA = CAP_B // 2 * BLOCK
B_ROWS = B_DATA + 8
A_DATA = CAP_A * BLOCK
A_ROWS = A_DATA + 8
WHERE = pl.BlockSpec(memory_space=pl.ANY)
IN_VMEM = pl.BlockSpec(memory_space=pltpu.VMEM)
BIG = 56 * 1024 * 1024
FIRST = 20 * 1024 * 1024
MIDDLE = 24 * 1024 * 1024
LAST = 16 * 1024 * 1024
IN_HBM = pl.BlockSpec(memory_space=pltpu.HBM)
IN_SMEM = pl.BlockSpec(memory_space=pltpu.SMEM)


def exchange(array, axis, step):
    mask = {0: (1, 3)[step], 1: (3, 1)[step]}
    route = [(2 * i + core, 2 * (i ^ mask[core]) + core) for i in range(4) for core in range(2)]
    return lax.ppermute(array, (axis, "core"), route)


def col_partner(place, core, distance):
    if distance == 4:
        return place ^ 4
    if distance == 2:
        forward = place // 2 % 2 == (core + place) % 2
        return (place + (2 if forward else -2)) % 8
    return (place + (1 if place % 2 == core else -1)) % 8


def exchange_col(array, distance):
    route = [(2 * i + core, 2 * col_partner(i, core, distance) + core) for i in range(8) for core in range(2)]
    return lax.ppermute(array, ("col", "core"), route)


def holders(place, core):
    held = [place]
    for distance in (4, 2, 1):
        partner = holders_before(col_partner(place, core, distance), core, distance)
        held = held + partner
    return held


def holders_before(place, core, distance):
    held = [place]
    for earlier in (4, 2):
        if earlier <= distance:
            break
        held = held + holders_before(col_partner(place, core, earlier), core, earlier)
    return held


def swap(array, axis):
    return lax.ppermute(array, axis, [(0, 1), (1, 0)])


def slot_at(places, count, cols, base):
    slots = places.shape[1]
    spot = places[0:1, :] * cols + places[1:2, :] + base
    position = lax.broadcasted_iota(jnp.int32, (LANES, slots), 0)
    slot = lax.broadcasted_iota(jnp.int32, (LANES, slots), 1)
    hit = (position == spot) & (slot < count)
    return jnp.max(jnp.where(hit, slot + 1, 0), axis=1, keepdims=True)


def as_rows(column):
    return jnp.transpose(jnp.broadcast_to(column.astype(jnp.float32), (LANES, LANES)))[0:8, :]


def pack_kernel(*refs):
    ins, (a_ref, b_ref), held, sems = refs[:6], refs[6:8], refs[8:14], refs[14]
    an_ref, bn_ref, ap_ref, bp_ref, bv_ref, av_ref = held
    copies = [pltpu.make_async_copy(ins[k], held[k], sems.at[k]) for k in range(6)]
    for copy in copies:
        copy.start()
    for copy in copies[:4]:
        copy.wait()
    copy_b, copy_a = copies[4:]
    spots = slot_at(ap_ref[0], an_ref[0], INNER, 0) + slot_at(ap_ref[1], an_ref[1], INNER, 16) - 1
    a_ref[A_DATA:, :] = as_rows(spots)
    spots = slot_at(bp_ref[...], bn_ref[0, 0, 0], COLS_B, 0) - 1
    b_ref[B_DATA:, :] = as_rows(spots)
    copy_b.wait()
    for pair in range(CAP_B // 2):
        b_ref[pair * BLOCK : (pair + 1) * BLOCK, :] = jnp.concatenate(
            [bv_ref[2 * pair], bv_ref[2 * pair + 1]], axis=1
        )
    copy_a.wait()
    for pair in range(CAP_A):
        a_ref[pair * BLOCK : (pair + 1) * BLOCK, :] = jnp.concatenate(
            [av_ref[2 * pair], av_ref[2 * pair + 1]], axis=1
        )


def pack(an, bn, ap, bp, bv, av):
    return pl.pallas_call(
        pack_kernel,
        out_shape=(
            jax.ShapeDtypeStruct((A_ROWS, LANES), jnp.float32),
            jax.ShapeDtypeStruct((B_ROWS, LANES), jnp.float32),
        ),
        in_specs=[IN_HBM] * 6,
        out_specs=(IN_VMEM, IN_VMEM),
        scratch_shapes=[
            pltpu.SMEM(an.shape, jnp.int32),
            pltpu.SMEM(bn.shape, jnp.int32),
            pltpu.VMEM(ap.shape, jnp.int32),
            pltpu.VMEM(bp.shape, jnp.int32),
            pltpu.VMEM(bv.shape, jnp.float32),
            pltpu.VMEM(av.shape, jnp.float32),
            pltpu.SemaphoreType.DMA((6,)),
        ],
        compiler_params=pltpu.CompilerParams(vmem_limit_bytes=BIG),
    )(an, bn, ap, bp, bv, av)


HELD = ((0,), (4,), (1,), (8, 12), (2, 3), (5, 9, 13), (6, 10, 14), (7, 11, 15))
CALLS = ((0, 1, 12, 2, 3), (4, 8, 13, 14, 5, 9, 6, 10), (15, 7, 11))
PLACED = ((0, 1, 12, 2, 3, 4, 8), (13, 14, 5, 9, 6, 10), (15, 7, 11))
AHEAD = 2 * LANES
NEAR = (0, 1, 12, 2, 3, 13, 14, 15)
LATE = CALLS[1] + CALLS[2]
FIRST_DEPTH, MIDDLE_DEPTH, LAST_DEPTH = (len(tiles) * LANES for tiles in CALLS)


def block_pair(load, left, right):
    lane = lax.broadcasted_iota(jnp.int32, (BLOCK, LANES), 1)
    low = jnp.maximum(left, 0)
    high = jnp.maximum(right, 0)
    one = pltpu.roll(load(low >> 1), (low & 1) * BLOCK, 1)
    two = pltpu.roll(load(high >> 1), (1 - (high & 1)) * BLOCK, 1)
    one = jnp.where((lane < BLOCK) & (left >= 0), one, 0.0)
    return jnp.where((lane >= BLOCK) & (right >= 0), two, one)


def halves(value):
    top = value.astype(jnp.bfloat16)
    return top, (value - top.astype(jnp.float32)).astype(jnp.bfloat16)


def ring_place(mask, core):
    near = jnp.where(mask == 1 + 2 * core, 1, 2)
    return jnp.where(mask == 0, 0, jnp.where(mask == 2, 3, near))


def place_left(me_ref, first, a_f, spots_s, a_hi, a_lo):
    x, zh, col, zl, core = (me_ref[k] for k in range(5))

    def left_tile(index, _):
        source = index // 2
        slot = index % 2
        holder = me_ref[5 + PIECES + (2 * col + core) * 8 + first + source]
        owner = (4 * x + zh + holder + 8 * slot + PIECES - col) % PIECES
        dx = ring_place((owner // 4) ^ x, core)
        dz = ring_place((owner % 4) ^ zh, core)
        at = me_ref[5 + 4 * dz + dx]
        lanes = pl.ds(pl.multiple_of(at * LANES, LANES), LANES)
        for r in range(ROWS_A):
            quarter = r // 2
            place = jnp.where(quarter % 2 == core, 2, 0) + jnp.where(quarter // 2 == zl, 1, 0)
            rows = pl.ds(pl.multiple_of(place * 128 + (r % 2) * BLOCK, BLOCK), BLOCK)

            def load(pair):
                return a_f[source, pl.ds(pl.multiple_of((slot * 4 + pair) * BLOCK, BLOCK), BLOCK), :]

            left = spots_s[source, slot * 16 + 2 * r].astype(jnp.int32)
            right = spots_s[source, slot * 16 + 2 * r + 1].astype(jnp.int32)
            a_hi[rows, lanes], a_lo[rows, lanes] = halves(block_pair(load, left, right))
        return 0

    lax.fori_loop(0, 8, left_tile, 0, unroll=2)


def right_copies(call, b_in, b_f, spots_s, sem_b, sem_s):
    tiles = PLACED[call]
    copies, spots = [], []
    for source, held in zip(b_in, [held for held in HELD if set(held) & set(tiles)], strict=True):
        for k, tile in enumerate(held):
            if tile not in tiles:
                continue
            at = tiles.index(tile)
            rows = pl.ds(k * B_ROWS, B_ROWS)
            copies.append(pltpu.make_async_copy(source.at[rows], b_f.at[at], sem_b.at[at]))
            spots.append(pltpu.make_async_copy(source.at[k * B_ROWS + B_DATA], spots_s.at[at], sem_s.at[at]))
    return copies, spots


def place_right(first, tiles, b_f, spots_s, b_hi, b_lo):
    def right_tile(tile, _):
        for k in range(INNER):
            rows = pl.ds(pl.multiple_of(tile * LANES + k * BLOCK, BLOCK), BLOCK)
            for c in range(COLS_B // 2):

                def load(pair):
                    return b_f[first + tile, pl.ds(pl.multiple_of(pair * BLOCK, BLOCK), BLOCK), :]

                spot = k * COLS_B + 2 * c
                left = spots_s[first + tile, spot].astype(jnp.int32)
                right = spots_s[first + tile, spot + 1].astype(jnp.int32)
                lanes = slice(c * LANES, (c + 1) * LANES)
                b_hi[rows, lanes], b_lo[rows, lanes] = halves(block_pair(load, left, right))
        return 0

    lax.fori_loop(0, tiles, right_tile, 0, unroll=3 if tiles == 3 else 2 - tiles % 2)


def left_copies(parts, a_f, spots_s, sem_a, sem_s):
    copies, spots = [], []
    for n, (part, k) in enumerate([(part, k) for part in parts for k in range(part.shape[0] // A_ROWS)]):
        copies.append(pltpu.make_async_copy(part.at[pl.ds(k * A_ROWS, A_ROWS)], a_f.at[n], sem_a.at[n]))
        spots.append(pltpu.make_async_copy(part.at[k * A_ROWS + A_DATA], spots_s.at[n], sem_s.at[n]))
    return copies, spots


def partial_product(left_hi, left_lo, b_hi, b_lo, store):
    for n in range(4):
        lanes = slice(n * 256, (n + 1) * 256)
        top = b_hi[:, lanes]
        total = jnp.dot(left_lo, top, preferred_element_type=jnp.float32)
        total += jnp.dot(left_hi, b_lo[:, lanes], preferred_element_type=jnp.float32)
        total += jnp.dot(left_hi, top, preferred_element_type=jnp.float32)
        store(lanes, total)


def early_kernel(n_right, *refs):
    b_in = refs[:n_right]
    b_hi, b_lo, ahead_hi, ahead_lo, b_f, spots_b, sem_b, sem_s = refs[n_right:]
    copies, spots = right_copies(0, b_in, b_f, spots_b, sem_b, sem_s)
    for copy in spots + copies:
        copy.start()
    for copy in spots + copies:
        copy.wait()
    place_right(0, len(CALLS[0]), b_f, spots_b, b_hi, b_lo)
    place_right(len(CALLS[0]), 2, b_f, spots_b, ahead_hi, ahead_lo)


def first_kernel(*refs):
    me_ref, a_in, b_in = refs[0], refs[1:4], refs[4:6]
    near_hi, near_lo, c_out = refs[6:9]
    a_f, spots_a, sem_a, sem_sa, b_hi, b_lo, sem_b = refs[9:]
    copies_a, spots_of_a = left_copies(a_in, a_f, spots_a, sem_a, sem_sa)
    copies = [pltpu.make_async_copy(b_in[k], (b_hi, b_lo)[k], sem_b.at[k]) for k in range(2)]
    for copy in spots_of_a + copies_a + copies:
        copy.start()
    for copy in spots_of_a + copies_a:
        copy.wait()
    place_left(me_ref, 0, a_f, spots_a, near_hi, near_lo)
    for copy in copies:
        copy.wait()

    def store(lanes, total):
        c_out[:, lanes] = total

    partial_product(near_hi[:, :FIRST_DEPTH], near_lo[:, :FIRST_DEPTH], b_hi, b_lo, store)


def middle_kernel(n_right, *refs):
    me_ref, a_in, near, c_in, ahead, b_in = refs[0], refs[1], refs[2:4], refs[4], refs[5:7], refs[7 : 7 + n_right]
    late_hi, late_lo, c_out = refs[7 + n_right : 10 + n_right]
    a_f, spots_a, sem_a, sem_sa, c_held, sem_c, b_f, b_hi, b_lo, spots_b, sem_b, sem_s = refs[10 + n_right :]
    copies_a, spots_of_a = left_copies((a_in,), a_f, spots_a, sem_a, sem_sa)
    copies, spots = right_copies(1, b_in, b_f, spots_b, sem_b, sem_s)
    held = [pltpu.make_async_copy(c_in, c_held, sem_c.at[0])]
    for k, dense in enumerate((b_hi, b_lo)):
        held.append(pltpu.make_async_copy(ahead[k], dense.at[pl.ds(0, AHEAD)], sem_c.at[5 + k]))
    for k, late in enumerate((late_hi, late_lo)):
        for n, (first, at, lanes) in enumerate(((FIRST_DEPTH, AHEAD, 256), (FIRST_DEPTH + 256, MIDDLE_DEPTH, 128))):
            source = near[k].at[:, pl.ds(first, lanes)]
            held.append(pltpu.make_async_copy(source, late.at[:, pl.ds(at, lanes)], sem_c.at[1 + 2 * k + n]))
    for copy in spots_of_a + copies_a + spots + copies + held:
        copy.start()
    for copy in spots_of_a + copies_a:
        copy.wait()
    place_left(me_ref, 4, a_f, spots_a, late_hi, late_lo)
    for copy in spots + copies:
        copy.wait()
    rest = pl.ds(AHEAD, MIDDLE_DEPTH - AHEAD)
    place_right(0, len(PLACED[1]), b_f, spots_b, b_hi.at[rest], b_lo.at[rest])
    for copy in held:
        copy.wait()

    def store(lanes, total):
        c_out[:, lanes] = total + c_held[:, lanes]

    partial_product(late_hi[:, :MIDDLE_DEPTH], late_lo[:, :MIDDLE_DEPTH], b_hi, b_lo, store)


def last_kernel(n_right, *refs):
    late_hi, late_lo, c_in = refs[:3]
    b_in = refs[3 : 3 + n_right]
    other, send, keep, b_f, b_hi, b_lo, spots_b, sem_b, sem_s = refs[3 + n_right :]
    copies, spots = right_copies(2, b_in, b_f, spots_b, sem_b, sem_s)
    for copy in spots + copies:
        copy.start()
    for copy in spots + copies:
        copy.wait()
    place_right(0, len(CALLS[2]), b_f, spots_b, b_hi, b_lo)

    def store(lanes, total):
        total += c_in[:, lanes]
        other[:, lanes] = total[:256]
        send[:, lanes] = total[256:384]
        keep[:, lanes] = total[384:]

    partial_product(late_hi[:, MIDDLE_DEPTH:], late_lo[:, MIDDLE_DEPTH:], b_hi, b_lo, store)


def right_scratch(call):
    tiles, depth = len(PLACED[call]), len(CALLS[call]) * LANES
    return [
        pltpu.VMEM((tiles, B_ROWS, LANES), jnp.float32),
        pltpu.VMEM((depth, 1024), jnp.bfloat16),
        pltpu.VMEM((depth, 1024), jnp.bfloat16),
        pltpu.SMEM((tiles, LANES), jnp.float32),
        pltpu.SemaphoreType.DMA((tiles,)),
        pltpu.SemaphoreType.DMA((tiles,)),
    ]


def used_by(call, b_all):
    return [b_all[k] for k in range(len(HELD)) if set(HELD[k]) & set(PLACED[call])]


def cost(call):
    flops = 3 * 2 * 512 * 1024 * LANES * len(CALLS[call])
    return pl.CostEstimate(flops=flops, bytes_accessed=16 * 1024 * 1024, transcendentals=0)


LEFT_SCRATCH = (
    pltpu.VMEM((4, A_ROWS, LANES), jnp.float32),
    pltpu.SMEM((4, LANES), jnp.float32),
    pltpu.SemaphoreType.DMA((4,)),
    pltpu.SemaphoreType.DMA((4,)),
)


def early_right(b_all):
    operands = used_by(0, b_all)
    dense = jax.ShapeDtypeStruct((FIRST_DEPTH, 1024), jnp.bfloat16)
    ahead = jax.ShapeDtypeStruct((AHEAD, 1024), jnp.bfloat16)
    scratch = right_scratch(0)
    return pl.pallas_call(
        lambda *refs: early_kernel(len(operands), *refs),
        out_shape=(dense, dense, ahead, ahead),
        in_specs=[WHERE] * len(operands),
        out_specs=(IN_VMEM,) * 4,
        scratch_shapes=scratch[:1] + scratch[3:],
        compiler_params=pltpu.CompilerParams(vmem_limit_bytes=FIRST),
        cost_estimate=pl.CostEstimate(flops=10**9, bytes_accessed=16 * 1024 * 1024, transcendentals=0),
    )(*operands)


def first_product(me, a_near, right):
    near = jax.ShapeDtypeStruct((512, len(NEAR) * LANES), jnp.bfloat16)
    return pl.pallas_call(
        first_kernel,
        out_shape=(near, near, jax.ShapeDtypeStruct((512, 1024), jnp.float32)),
        in_specs=[IN_SMEM] + [WHERE] * 5,
        out_specs=(IN_VMEM,) * 3,
        scratch_shapes=[*LEFT_SCRATCH, *right_scratch(0)[1:3], pltpu.SemaphoreType.DMA((2,))],
        compiler_params=pltpu.CompilerParams(vmem_limit_bytes=FIRST),
        cost_estimate=cost(0),
    )(me, *a_near, *right)


def middle_product(me, a_far, near_hi, near_lo, so_far, ahead, b_all):
    operands = used_by(1, b_all)
    late = jax.ShapeDtypeStruct((512, len(LATE) * LANES), jnp.bfloat16)
    return pl.pallas_call(
        lambda *refs: middle_kernel(len(operands), *refs),
        out_shape=(late, late, jax.ShapeDtypeStruct((512, 1024), jnp.float32)),
        in_specs=[IN_SMEM] + [WHERE] * (6 + len(operands)),
        out_specs=(IN_VMEM,) * 3,
        scratch_shapes=[
            *LEFT_SCRATCH,
            pltpu.VMEM((512, 1024), jnp.float32),
            pltpu.SemaphoreType.DMA((7,)),
            *right_scratch(1),
        ],
        compiler_params=pltpu.CompilerParams(vmem_limit_bytes=MIDDLE),
        cost_estimate=cost(1),
    )(me, a_far, near_hi, near_lo, so_far, *ahead, *operands)


def last_product(late_hi, late_lo, so_far, b_all):
    operands = used_by(2, b_all)
    return pl.pallas_call(
        lambda *refs: last_kernel(len(operands), *refs),
        out_shape=tuple(jax.ShapeDtypeStruct((rows, 1024), jnp.float32) for rows in (256, 128, 128)),
        in_specs=[IN_VMEM] * 3 + [WHERE] * len(operands),
        out_specs=(IN_VMEM,) * 3,
        scratch_shapes=right_scratch(2),
        compiler_params=pltpu.CompilerParams(vmem_limit_bytes=LAST),
        cost_estimate=cost(2),
    )(late_hi, late_lo, so_far, *operands)


def body(a_values, a_places, a_counts, b_values, b_places, b_counts):
    hold = lax.optimization_barrier
    by_place = [holder for place in range(8) for core in range(2) for holder in holders(place, core)]
    me = [lax.axis_index(name) for name in ("x", "zh", "col", "zl", "core")]
    table = jnp.array([(NEAR if tile in NEAR else LATE).index(tile) for tile in range(PIECES)] + by_place, jnp.int32)
    me = jnp.concatenate([jnp.stack(me).astype(jnp.int32), table])
    own_a, own = pack(
        a_counts.reshape(2),
        b_counts,
        a_places.reshape(2, CAP_A, 2).swapaxes(1, 2),
        b_places.reshape(CAP_B, 2).swapaxes(0, 1),
        b_values.reshape(CAP_B, BLOCK, BLOCK),
        a_values.reshape(2 * CAP_A, BLOCK, BLOCK),
    )
    z_one = exchange(own, "zh", 0)
    x_one = exchange(own, "x", 0)
    z_one, own_a = hold((z_one, own_a))
    a_one = exchange_col(own_a, 4)

    z_two = exchange(jnp.concatenate([own, z_one, own[:8]], axis=0), "zh", 1)
    x_two = exchange(jnp.concatenate([own, x_one], axis=0), "x", 1)
    x_two, z_two = hold((x_two, z_two))
    a_one, _ = hold((a_one, z_two))
    a_two = exchange_col(jnp.concatenate([own_a, a_one], axis=0), 2)

    column = jnp.concatenate([z_one, z_two[: 2 * B_ROWS]], axis=0)
    x_three = exchange(column, "x", 0)
    x_four = exchange(column, "x", 1)
    b_all = [own, z_one, x_one, z_two, x_two]
    right = early_right(b_all)
    a_two, *right = hold((a_two, *right))
    a_four = exchange_col(jnp.concatenate([own_a, a_one, a_two], axis=0), 1)
    x_three, a_two = hold((x_three, a_two))
    near_hi, near_lo, total = first_product(me, (own_a, a_one, a_two), right[:2])
    b_all += [x_three, x_four, exchange(x_three, "x", 1)]
    late_hi, late_lo, total = middle_product(me, a_four, near_hi, near_lo, total, right[2:], b_all)
    other, send, keep = last_product(late_hi, late_lo, total, b_all)

    got = swap(other, "core")
    ahead = swap(send + got[:128], "zl")
    return (keep + got[128:]) + ahead


def solution(mesh):
    split = Mesh(mesh.devices.reshape(4, 4, 8, 2, 2), ("x", "zh", "col", "zl", "core"))
    row, layer = ("x", "zh"), ("zl", "core")
    in_specs = (
        P(row, "col", layer, None, None, None, None),
        P(row, "col", layer, None, None, None),
        P(row, "col", layer, None),
        P(row, "col", layer, None, None, None),
        P(row, "col", layer, None, None),
        P(row, "col", layer),
    )
    out_specs = P(("x", "zh", "zl", "core"), "col")
    return jax.shard_map(body, mesh=split, in_specs=in_specs, out_specs=out_specs, check_vma=False)
```

```python
import jax
import jax.numpy as jnp
from jax import lax
from jax.experimental import pallas as pl
from jax.experimental.pallas import tpu as pltpu
from jax.sharding import Mesh, PartitionSpec as P

BLOCK = 64
LANES = 128
CAP_A = 8
CAP_B = 24
ROWS_A = 8
INNER = 2
COLS_B = 16
PIECES = 16
B_DATA = CAP_B // 2 * BLOCK
B_ROWS = B_DATA + 8
A_DATA = CAP_A * BLOCK
A_ROWS = A_DATA + 8
WHERE = pl.BlockSpec(memory_space=pl.ANY)
IN_VMEM = pl.BlockSpec(memory_space=pltpu.VMEM)
BIG = 56 * 1024 * 1024
FIRST = 20 * 1024 * 1024
MIDDLE = 24 * 1024 * 1024
LAST = 16 * 1024 * 1024
IN_HBM = pl.BlockSpec(memory_space=pltpu.HBM)
IN_SMEM = pl.BlockSpec(memory_space=pltpu.SMEM)


def exchange(array, axis, step):
    mask = {0: (1, 3)[step], 1: (3, 1)[step]}
    route = [(2 * i + core, 2 * (i ^ mask[core]) + core) for i in range(4) for core in range(2)]
    return lax.ppermute(array, (axis, "core"), route)


def col_partner(place, core, distance):
    if distance == 4:
        return place ^ 4
    if distance == 2:
        forward = place // 2 % 2 == (core + place) % 2
        return (place + (2 if forward else -2)) % 8
    return (place + (1 if place % 2 == core else -1)) % 8


def exchange_col(array, distance):
    route = [(2 * i + core, 2 * col_partner(i, core, distance) + core) for i in range(8) for core in range(2)]
    return lax.ppermute(array, ("col", "core"), route)


def holders(place, core):
    held = [place]
    for distance in (4, 2, 1):
        partner = holders_before(col_partner(place, core, distance), core, distance)
        held = held + partner
    return held


def holders_before(place, core, distance):
    held = [place]
    for earlier in (4, 2):
        if earlier <= distance:
            break
        held = held + holders_before(col_partner(place, core, earlier), core, earlier)
    return held


def swap(array, axis):
    return lax.ppermute(array, axis, [(0, 1), (1, 0)])


def slot_at(places, count, cols, base):
    slots = places.shape[1]
    spot = places[0:1, :] * cols + places[1:2, :] + base
    position = lax.broadcasted_iota(jnp.int32, (LANES, slots), 0)
    slot = lax.broadcasted_iota(jnp.int32, (LANES, slots), 1)
    hit = (position == spot) & (slot < count)
    return jnp.max(jnp.where(hit, slot + 1, 0), axis=1, keepdims=True)


def as_rows(column):
    return jnp.transpose(jnp.broadcast_to(column.astype(jnp.float32), (LANES, LANES)))[0:8, :]


def pack_kernel(*refs):
    ins, (a_ref, b_ref), held, sems = refs[:6], refs[6:8], refs[8:14], refs[14]
    an_ref, bn_ref, ap_ref, bp_ref, bv_ref, av_ref = held
    copies = [pltpu.make_async_copy(ins[k], held[k], sems.at[k]) for k in range(6)]
    for copy in copies:
        copy.start()
    for copy in copies[:4]:
        copy.wait()
    copy_b, copy_a = copies[4:]
    spots = slot_at(ap_ref[0], an_ref[0], INNER, 0) + slot_at(ap_ref[1], an_ref[1], INNER, 16) - 1
    a_ref[A_DATA:, :] = as_rows(spots)
    spots = slot_at(bp_ref[...], bn_ref[0, 0, 0], COLS_B, 0) - 1
    b_ref[B_DATA:, :] = as_rows(spots)
    copy_b.wait()
    for pair in range(CAP_B // 2):
        b_ref[pair * BLOCK : (pair + 1) * BLOCK, :] = jnp.concatenate(
            [bv_ref[2 * pair], bv_ref[2 * pair + 1]], axis=1
        )
    copy_a.wait()
    for pair in range(CAP_A):
        a_ref[pair * BLOCK : (pair + 1) * BLOCK, :] = jnp.concatenate(
            [av_ref[2 * pair], av_ref[2 * pair + 1]], axis=1
        )


def pack(an, bn, ap, bp, bv, av):
    return pl.pallas_call(
        pack_kernel,
        out_shape=(
            jax.ShapeDtypeStruct((A_ROWS, LANES), jnp.float32),
            jax.ShapeDtypeStruct((B_ROWS, LANES), jnp.float32),
        ),
        in_specs=[IN_HBM] * 6,
        out_specs=(IN_VMEM, IN_VMEM),
        scratch_shapes=[
            pltpu.SMEM(an.shape, jnp.int32),
            pltpu.SMEM(bn.shape, jnp.int32),
            pltpu.VMEM(ap.shape, jnp.int32),
            pltpu.VMEM(bp.shape, jnp.int32),
            pltpu.VMEM(bv.shape, jnp.float32),
            pltpu.VMEM(av.shape, jnp.float32),
            pltpu.SemaphoreType.DMA((6,)),
        ],
        compiler_params=pltpu.CompilerParams(vmem_limit_bytes=BIG),
    )(an, bn, ap, bp, bv, av)


HELD = ((0,), (4,), (1,), (8, 12), (2, 3), (5, 9, 13), (6, 10, 14), (7, 11, 15))
CALLS = ((0, 1, 12, 2, 3), (4, 8, 13, 14, 5, 9, 6, 10), (15, 7, 11))
PLACED = ((0, 1, 12, 2, 3, 4, 8), (13, 14, 5, 9, 6, 10), (15, 7, 11))
AHEAD = 2 * LANES
NEAR = (0, 1, 12, 2, 3, 13, 14, 15)
LATE = CALLS[1] + CALLS[2]
FIRST_DEPTH, MIDDLE_DEPTH, LAST_DEPTH = (len(tiles) * LANES for tiles in CALLS)


def block_pair(load, left, right):
    lane = lax.broadcasted_iota(jnp.int32, (BLOCK, LANES), 1)
    low = jnp.maximum(left, 0)
    high = jnp.maximum(right, 0)
    one = pltpu.roll(load(low >> 1), (low & 1) * BLOCK, 1)
    two = pltpu.roll(load(high >> 1), (1 - (high & 1)) * BLOCK, 1)
    one = jnp.where((lane < BLOCK) & (left >= 0), one, 0.0)
    return jnp.where((lane >= BLOCK) & (right >= 0), two, one)


def halves(value):
    top = value.astype(jnp.bfloat16)
    return top, (value - top.astype(jnp.float32)).astype(jnp.bfloat16)


def ring_place(mask, core):
    near = jnp.where(mask == 1 + 2 * core, 1, 2)
    return jnp.where(mask == 0, 0, jnp.where(mask == 2, 3, near))


def place_left(me_ref, first, a_f, spots_s, a_hi, a_lo):
    x, zh, col, zl, core = (me_ref[k] for k in range(5))

    def left_tile(index, _):
        source = index // 2
        slot = index % 2
        holder = me_ref[5 + PIECES + (2 * col + core) * 8 + first + source]
        owner = (4 * x + zh + holder + 8 * slot + PIECES - col) % PIECES
        dx = ring_place((owner // 4) ^ x, core)
        dz = ring_place((owner % 4) ^ zh, core)
        at = me_ref[5 + 4 * dz + dx]
        lanes = pl.ds(pl.multiple_of(at * LANES, LANES), LANES)
        for r in range(ROWS_A):
            quarter = r // 2
            place = jnp.where(quarter % 2 == core, 2, 0) + jnp.where(quarter // 2 == zl, 1, 0)
            rows = pl.ds(pl.multiple_of(place * 128 + (r % 2) * BLOCK, BLOCK), BLOCK)

            def load(pair):
                return a_f[source, pl.ds(pl.multiple_of((slot * 4 + pair) * BLOCK, BLOCK), BLOCK), :]

            left = spots_s[source, slot * 16 + 2 * r].astype(jnp.int32)
            right = spots_s[source, slot * 16 + 2 * r + 1].astype(jnp.int32)
            a_hi[rows, lanes], a_lo[rows, lanes] = halves(block_pair(load, left, right))
        return 0

    lax.fori_loop(0, 8, left_tile, 0, unroll=2)


def right_copies(call, b_in, b_f, spots_s, sem_b, sem_s):
    tiles = PLACED[call]
    copies, spots = [], []
    for source, held in zip(b_in, [held for held in HELD if set(held) & set(tiles)], strict=True):
        for k, tile in enumerate(held):
            if tile not in tiles:
                continue
            at = tiles.index(tile)
            rows = pl.ds(k * B_ROWS, B_ROWS)
            copies.append(pltpu.make_async_copy(source.at[rows], b_f.at[at], sem_b.at[at]))
            spots.append(pltpu.make_async_copy(source.at[k * B_ROWS + B_DATA], spots_s.at[at], sem_s.at[at]))
    return copies, spots


def place_right(first, tiles, b_f, spots_s, b_hi, b_lo):
    def right_tile(tile, _):
        for k in range(INNER):
            rows = pl.ds(pl.multiple_of(tile * LANES + k * BLOCK, BLOCK), BLOCK)
            for c in range(COLS_B // 2):

                def load(pair):
                    return b_f[first + tile, pl.ds(pl.multiple_of(pair * BLOCK, BLOCK), BLOCK), :]

                spot = k * COLS_B + 2 * c
                left = spots_s[first + tile, spot].astype(jnp.int32)
                right = spots_s[first + tile, spot + 1].astype(jnp.int32)
                lanes = slice(c * LANES, (c + 1) * LANES)
                b_hi[rows, lanes], b_lo[rows, lanes] = halves(block_pair(load, left, right))
        return 0

    lax.fori_loop(0, tiles, right_tile, 0, unroll=3 if tiles == 3 else 2 - tiles % 2)


def left_copies(parts, a_f, spots_s, sem_a, sem_s):
    copies, spots = [], []
    for n, (part, k) in enumerate([(part, k) for part in parts for k in range(part.shape[0] // A_ROWS)]):
        copies.append(pltpu.make_async_copy(part.at[pl.ds(k * A_ROWS, A_ROWS)], a_f.at[n], sem_a.at[n]))
        spots.append(pltpu.make_async_copy(part.at[k * A_ROWS + A_DATA], spots_s.at[n], sem_s.at[n]))
    return copies, spots


def partial_product(left_hi, left_lo, b_hi, b_lo, store):
    for n in range(4):
        lanes = slice(n * 256, (n + 1) * 256)
        top = b_hi[:, lanes]
        total = jnp.dot(left_lo, top, preferred_element_type=jnp.float32)
        total += jnp.dot(left_hi, b_lo[:, lanes], preferred_element_type=jnp.float32)
        total += jnp.dot(left_hi, top, preferred_element_type=jnp.float32)
        store(lanes, total)


def early_kernel(n_right, *refs):
    b_in = refs[:n_right]
    b_hi, b_lo, ahead_hi, ahead_lo, b_f, spots_b, sem_b, sem_s = refs[n_right:]
    copies, spots = right_copies(0, b_in, b_f, spots_b, sem_b, sem_s)
    for copy in spots + copies:
        copy.start()
    for copy in spots + copies:
        copy.wait()
    place_right(0, len(CALLS[0]), b_f, spots_b, b_hi, b_lo)
    place_right(len(CALLS[0]), 2, b_f, spots_b, ahead_hi, ahead_lo)


def first_kernel(*refs):
    me_ref, a_in, b_in = refs[0], refs[1:4], refs[4:6]
    near_hi, near_lo, c_out = refs[6:9]
    a_f, spots_a, sem_a, sem_sa, b_hi, b_lo, sem_b = refs[9:]
    copies_a, spots_of_a = left_copies(a_in, a_f, spots_a, sem_a, sem_sa)
    copies = [pltpu.make_async_copy(b_in[k], (b_hi, b_lo)[k], sem_b.at[k]) for k in range(2)]
    for copy in spots_of_a + copies_a + copies:
        copy.start()
    for copy in spots_of_a + copies_a:
        copy.wait()
    place_left(me_ref, 0, a_f, spots_a, near_hi, near_lo)
    for copy in copies:
        copy.wait()

    def store(lanes, total):
        c_out[:, lanes] = total

    partial_product(near_hi[:, :FIRST_DEPTH], near_lo[:, :FIRST_DEPTH], b_hi, b_lo, store)


def middle_kernel(n_right, *refs):
    me_ref, a_in, near, c_in, ahead, b_in = refs[0], refs[1], refs[2:4], refs[4], refs[5:7], refs[7 : 7 + n_right]
    late_hi, late_lo, c_out = refs[7 + n_right : 10 + n_right]
    a_f, spots_a, sem_a, sem_sa, c_held, sem_c, b_f, b_hi, b_lo, spots_b, sem_b, sem_s = refs[10 + n_right :]
    copies_a, spots_of_a = left_copies((a_in,), a_f, spots_a, sem_a, sem_sa)
    copies, spots = right_copies(1, b_in, b_f, spots_b, sem_b, sem_s)
    held = [pltpu.make_async_copy(c_in, c_held, sem_c.at[0])]
    for k, dense in enumerate((b_hi, b_lo)):
        held.append(pltpu.make_async_copy(ahead[k], dense.at[pl.ds(0, AHEAD)], sem_c.at[5 + k]))
    for k, late in enumerate((late_hi, late_lo)):
        for n, (first, at, lanes) in enumerate(((FIRST_DEPTH, AHEAD, 256), (FIRST_DEPTH + 256, MIDDLE_DEPTH, 128))):
            source = near[k].at[:, pl.ds(first, lanes)]
            held.append(pltpu.make_async_copy(source, late.at[:, pl.ds(at, lanes)], sem_c.at[1 + 2 * k + n]))
    for copy in spots_of_a + copies_a + spots + copies + held:
        copy.start()
    for copy in spots_of_a + copies_a:
        copy.wait()
    place_left(me_ref, 4, a_f, spots_a, late_hi, late_lo)
    for copy in spots + copies:
        copy.wait()
    rest = pl.ds(AHEAD, MIDDLE_DEPTH - AHEAD)
    place_right(0, len(PLACED[1]), b_f, spots_b, b_hi.at[rest], b_lo.at[rest])
    for copy in held:
        copy.wait()

    def store(lanes, total):
        c_out[:, lanes] = total + c_held[:, lanes]

    partial_product(late_hi[:, :MIDDLE_DEPTH], late_lo[:, :MIDDLE_DEPTH], b_hi, b_lo, store)


def last_kernel(n_right, *refs):
    late_hi, late_lo, c_in = refs[:3]
    b_in = refs[3 : 3 + n_right]
    other, send, keep, b_f, b_hi, b_lo, spots_b, sem_b, sem_s = refs[3 + n_right :]
    copies, spots = right_copies(2, b_in, b_f, spots_b, sem_b, sem_s)
    for copy in spots + copies:
        copy.start()
    for copy in spots + copies:
        copy.wait()
    place_right(0, len(CALLS[2]), b_f, spots_b, b_hi, b_lo)

    def store(lanes, total):
        total += c_in[:, lanes]
        other[:, lanes] = total[:256]
        send[:, lanes] = total[256:384]
        keep[:, lanes] = total[384:]

    partial_product(late_hi[:, MIDDLE_DEPTH:], late_lo[:, MIDDLE_DEPTH:], b_hi, b_lo, store)


def right_scratch(call):
    tiles, depth = len(PLACED[call]), len(CALLS[call]) * LANES
    return [
        pltpu.VMEM((tiles, B_ROWS, LANES), jnp.float32),
        pltpu.VMEM((depth, 1024), jnp.bfloat16),
        pltpu.VMEM((depth, 1024), jnp.bfloat16),
        pltpu.SMEM((tiles, LANES), jnp.float32),
        pltpu.SemaphoreType.DMA((tiles,)),
        pltpu.SemaphoreType.DMA((tiles,)),
    ]


def used_by(call, b_all):
    return [b_all[k] for k in range(len(HELD)) if set(HELD[k]) & set(PLACED[call])]


def cost(call):
    flops = 3 * 2 * 512 * 1024 * LANES * len(CALLS[call])
    return pl.CostEstimate(flops=flops, bytes_accessed=16 * 1024 * 1024, transcendentals=0)


LEFT_SCRATCH = (
    pltpu.VMEM((4, A_ROWS, LANES), jnp.float32),
    pltpu.SMEM((4, LANES), jnp.float32),
    pltpu.SemaphoreType.DMA((4,)),
    pltpu.SemaphoreType.DMA((4,)),
)


def early_right(b_all):
    operands = used_by(0, b_all)
    dense = jax.ShapeDtypeStruct((FIRST_DEPTH, 1024), jnp.bfloat16)
    ahead = jax.ShapeDtypeStruct((AHEAD, 1024), jnp.bfloat16)
    scratch = right_scratch(0)
    return pl.pallas_call(
        lambda *refs: early_kernel(len(operands), *refs),
        out_shape=(dense, dense, ahead, ahead),
        in_specs=[WHERE] * len(operands),
        out_specs=(IN_VMEM,) * 4,
        scratch_shapes=scratch[:1] + scratch[3:],
        compiler_params=pltpu.CompilerParams(vmem_limit_bytes=FIRST),
        cost_estimate=pl.CostEstimate(flops=10**9, bytes_accessed=16 * 1024 * 1024, transcendentals=0),
    )(*operands)


def first_product(me, a_near, right):
    near = jax.ShapeDtypeStruct((512, len(NEAR) * LANES), jnp.bfloat16)
    return pl.pallas_call(
        first_kernel,
        out_shape=(near, near, jax.ShapeDtypeStruct((512, 1024), jnp.float32)),
        in_specs=[IN_SMEM] + [WHERE] * 5,
        out_specs=(IN_VMEM,) * 3,
        scratch_shapes=[*LEFT_SCRATCH, *right_scratch(0)[1:3], pltpu.SemaphoreType.DMA((2,))],
        compiler_params=pltpu.CompilerParams(vmem_limit_bytes=FIRST),
        cost_estimate=cost(0),
    )(me, *a_near, *right)


def middle_product(me, a_far, near_hi, near_lo, so_far, ahead, b_all):
    operands = used_by(1, b_all)
    late = jax.ShapeDtypeStruct((512, len(LATE) * LANES), jnp.bfloat16)
    return pl.pallas_call(
        lambda *refs: middle_kernel(len(operands), *refs),
        out_shape=(late, late, jax.ShapeDtypeStruct((512, 1024), jnp.float32)),
        in_specs=[IN_SMEM] + [WHERE] * (6 + len(operands)),
        out_specs=(IN_VMEM,) * 3,
        scratch_shapes=[
            *LEFT_SCRATCH,
            pltpu.VMEM((512, 1024), jnp.float32),
            pltpu.SemaphoreType.DMA((7,)),
            *right_scratch(1),
        ],
        compiler_params=pltpu.CompilerParams(vmem_limit_bytes=MIDDLE),
        cost_estimate=cost(1),
    )(me, a_far, near_hi, near_lo, so_far, *ahead, *operands)


def last_product(late_hi, late_lo, so_far, b_all):
    operands = used_by(2, b_all)
    return pl.pallas_call(
        lambda *refs: last_kernel(len(operands), *refs),
        out_shape=tuple(jax.ShapeDtypeStruct((rows, 1024), jnp.float32) for rows in (256, 128, 128)),
        in_specs=[IN_VMEM] * 3 + [WHERE] * len(operands),
        out_specs=(IN_VMEM,) * 3,
        scratch_shapes=right_scratch(2),
        compiler_params=pltpu.CompilerParams(vmem_limit_bytes=LAST),
        cost_estimate=cost(2),
    )(late_hi, late_lo, so_far, *operands)


def join_kernel(*refs):
    parts, out, sems = refs[:-2], refs[-2], refs[-1]
    copies, row = [], 0
    for k, part in enumerate(parts):
        copies.append(pltpu.make_async_copy(part, out.at[pl.ds(row, part.shape[0])], sems.at[k]))
        row += part.shape[0]
    for copy in copies:
        copy.start()
    for copy in copies:
        copy.wait()


def join(parts):
    rows = sum(part.shape[0] for part in parts)
    return pl.pallas_call(
        join_kernel,
        out_shape=jax.ShapeDtypeStruct((rows, LANES), jnp.float32),
        in_specs=[WHERE] * len(parts),
        out_specs=IN_VMEM,
        scratch_shapes=[pltpu.SemaphoreType.DMA((len(parts),))],
        compiler_params=pltpu.CompilerParams(vmem_limit_bytes=4 * 1024 * 1024),
    )(*parts)


def body(a_values, a_places, a_counts, b_values, b_places, b_counts):
    hold = lax.optimization_barrier
    by_place = [holder for place in range(8) for core in range(2) for holder in holders(place, core)]
    me = [lax.axis_index(name) for name in ("x", "zh", "col", "zl", "core")]
    table = jnp.array([(NEAR if tile in NEAR else LATE).index(tile) for tile in range(PIECES)] + by_place, jnp.int32)
    me = jnp.concatenate([jnp.stack(me).astype(jnp.int32), table])
    own_a, own = pack(
        a_counts.reshape(2),
        b_counts,
        a_places.reshape(2, CAP_A, 2).swapaxes(1, 2),
        b_places.reshape(CAP_B, 2).swapaxes(0, 1),
        b_values.reshape(CAP_B, BLOCK, BLOCK),
        a_values.reshape(2 * CAP_A, BLOCK, BLOCK),
    )
    z_one = exchange(own, "zh", 0)
    x_one = exchange(own, "x", 0)
    z_one, own_a, me = hold((z_one, own_a, me))
    a_one = exchange_col(own_a, 4)

    z_two = exchange(jnp.concatenate([own, z_one, own[:8]], axis=0), "zh", 1)
    x_two = exchange(jnp.concatenate([own, x_one], axis=0), "x", 1)
    x_two, z_two = hold((x_two, z_two))
    a_one, _ = hold((a_one, z_two))
    a_two = exchange_col(jnp.concatenate([own_a, a_one], axis=0), 2)

    column = jnp.concatenate([z_one, z_two[: 2 * B_ROWS]], axis=0)
    x_three = exchange(column, "x", 0)
    x_four = exchange(column, "x", 1)
    b_all = [own, z_one, x_one, z_two, x_two]
    right = early_right(b_all)
    a_two, *right = hold((a_two, *right))
    a_four = exchange_col(join([own_a, a_one, a_two]), 1)
    x_three, a_two = hold((x_three, a_two))
    near_hi, near_lo, total = first_product(me, (own_a, a_one, a_two), right[:2])
    b_all += [x_three, x_four, exchange(x_three, "x", 1)]
    late_hi, late_lo, total = middle_product(me, a_four, near_hi, near_lo, total, right[2:], b_all)
    other, send, keep = last_product(late_hi, late_lo, total, b_all)

    got = swap(other, "core")
    ahead = swap(send + got[:128], "zl")
    return (keep + got[128:]) + ahead


def solution(mesh):
    split = Mesh(mesh.devices.reshape(4, 4, 8, 2, 2), ("x", "zh", "col", "zl", "core"))
    row, layer = ("x", "zh"), ("zl", "core")
    in_specs = (
        P(row, "col", layer, None, None, None, None),
        P(row, "col", layer, None, None, None),
        P(row, "col", layer, None),
        P(row, "col", layer, None, None, None),
        P(row, "col", layer, None, None),
        P(row, "col", layer),
    )
    out_specs = P(("x", "zh", "zl", "core"), "col")
    return jax.shard_map(body, mesh=split, in_specs=in_specs, out_specs=out_specs, check_vma=False)
```

```python
import jax
import jax.numpy as jnp
from jax import lax
from jax.experimental import pallas as pl
from jax.experimental.pallas import tpu as pltpu
from jax.sharding import Mesh, PartitionSpec as P

BLOCK = 64
LANES = 128
CAP_A = 8
CAP_B = 24
ROWS_A = 8
INNER = 2
COLS_B = 16
PIECES = 16
B_DATA = CAP_B // 2 * BLOCK
B_ROWS = B_DATA + 8
A_DATA = CAP_A * BLOCK
A_ROWS = A_DATA + 8
WHERE = pl.BlockSpec(memory_space=pl.ANY)
IN_VMEM = pl.BlockSpec(memory_space=pltpu.VMEM)
BIG = 56 * 1024 * 1024
FIRST = 20 * 1024 * 1024
MIDDLE = 24 * 1024 * 1024
LAST = 16 * 1024 * 1024
IN_HBM = pl.BlockSpec(memory_space=pltpu.HBM)
IN_SMEM = pl.BlockSpec(memory_space=pltpu.SMEM)


def exchange(array, axis, step):
    mask = {0: (1, 3)[step], 1: (3, 1)[step]}
    route = [(2 * i + core, 2 * (i ^ mask[core]) + core) for i in range(4) for core in range(2)]
    return lax.ppermute(array, (axis, "core"), route)


def col_partner(place, core, distance):
    if distance == 4:
        return place ^ 4
    if distance == 2:
        forward = place // 2 % 2 == (core + place) % 2
        return (place + (2 if forward else -2)) % 8
    return (place + (1 if place % 2 == core else -1)) % 8


def exchange_col(array, distance):
    route = [(2 * i + core, 2 * col_partner(i, core, distance) + core) for i in range(8) for core in range(2)]
    return lax.ppermute(array, ("col", "core"), route)


def holders(place, core):
    held = [place]
    for distance in (4, 2, 1):
        partner = holders_before(col_partner(place, core, distance), core, distance)
        held = held + partner
    return held


def holders_before(place, core, distance):
    held = [place]
    for earlier in (4, 2):
        if earlier <= distance:
            break
        held = held + holders_before(col_partner(place, core, earlier), core, earlier)
    return held


def swap(array, axis):
    return lax.ppermute(array, axis, [(0, 1), (1, 0)])


def slot_at(places, count, cols, base):
    slots = places.shape[1]
    spot = places[0:1, :] * cols + places[1:2, :] + base
    position = lax.broadcasted_iota(jnp.int32, (LANES, slots), 0)
    slot = lax.broadcasted_iota(jnp.int32, (LANES, slots), 1)
    hit = (position == spot) & (slot < count)
    return jnp.max(jnp.where(hit, slot + 1, 0), axis=1, keepdims=True)


def as_rows(column):
    return jnp.transpose(jnp.broadcast_to(column.astype(jnp.float32), (LANES, LANES)))[0:8, :]


def pack_kernel(*refs):
    ins, (a_ref, b_ref), held, sems = refs[:6], refs[6:8], refs[8:14], refs[14]
    an_ref, bn_ref, ap_ref, bp_ref, bv_ref, av_ref = held
    copies = [pltpu.make_async_copy(ins[k], held[k], sems.at[k]) for k in range(6)]
    for copy in copies:
        copy.start()
    for copy in copies[:4]:
        copy.wait()
    copy_b, copy_a = copies[4:]
    spots = slot_at(ap_ref[0], an_ref[0], INNER, 0) + slot_at(ap_ref[1], an_ref[1], INNER, 16) - 1
    a_ref[A_DATA:, :] = as_rows(spots)
    spots = slot_at(bp_ref[...], bn_ref[0, 0, 0], COLS_B, 0) - 1
    b_ref[B_DATA:, :] = as_rows(spots)
    copy_b.wait()
    for pair in range(CAP_B // 2):
        b_ref[pair * BLOCK : (pair + 1) * BLOCK, :] = jnp.concatenate(
            [bv_ref[2 * pair], bv_ref[2 * pair + 1]], axis=1
        )
    copy_a.wait()
    for pair in range(CAP_A):
        a_ref[pair * BLOCK : (pair + 1) * BLOCK, :] = jnp.concatenate(
            [av_ref[2 * pair], av_ref[2 * pair + 1]], axis=1
        )


def pack(an, bn, ap, bp, bv, av):
    return pl.pallas_call(
        pack_kernel,
        out_shape=(
            jax.ShapeDtypeStruct((A_ROWS, LANES), jnp.float32),
            jax.ShapeDtypeStruct((B_ROWS, LANES), jnp.float32),
        ),
        in_specs=[IN_HBM] * 6,
        out_specs=(IN_VMEM, IN_VMEM),
        scratch_shapes=[
            pltpu.SMEM(an.shape, jnp.int32),
            pltpu.SMEM(bn.shape, jnp.int32),
            pltpu.VMEM(ap.shape, jnp.int32),
            pltpu.VMEM(bp.shape, jnp.int32),
            pltpu.VMEM(bv.shape, jnp.float32),
            pltpu.VMEM(av.shape, jnp.float32),
            pltpu.SemaphoreType.DMA((6,)),
        ],
        compiler_params=pltpu.CompilerParams(vmem_limit_bytes=BIG),
    )(an, bn, ap, bp, bv, av)


HELD = ((0,), (4,), (1,), (8, 12), (2, 3), (5, 9, 13), (6, 10, 14), (7, 11, 15))
CALLS = ((0, 1, 12, 2, 3), (4, 8, 13, 14, 5, 9, 6, 10), (15, 7, 11))
PLACED = ((0, 1, 12, 2, 3, 4, 8), (13, 14, 5, 9, 6, 10), (15, 7, 11))
AHEAD = 2 * LANES
NEAR = (0, 1, 12, 2, 3, 13, 14, 15)
LATE = CALLS[1] + CALLS[2]
FIRST_DEPTH, MIDDLE_DEPTH, LAST_DEPTH = (len(tiles) * LANES for tiles in CALLS)


def block_pair(load, left, right):
    lane = lax.broadcasted_iota(jnp.int32, (BLOCK, LANES), 1)
    low = jnp.maximum(left, 0)
    high = jnp.maximum(right, 0)
    one = pltpu.roll(load(low >> 1), (low & 1) * BLOCK, 1)
    two = pltpu.roll(load(high >> 1), (1 - (high & 1)) * BLOCK, 1)
    one = jnp.where((lane < BLOCK) & (left >= 0), one, 0.0)
    return jnp.where((lane >= BLOCK) & (right >= 0), two, one)


def halves(value):
    top = value.astype(jnp.bfloat16)
    return top, (value - top.astype(jnp.float32)).astype(jnp.bfloat16)


def ring_place(mask, core):
    near = jnp.where(mask == 1 + 2 * core, 1, 2)
    return jnp.where(mask == 0, 0, jnp.where(mask == 2, 3, near))


def place_left(me_ref, first, a_f, spots_s, a_hi, a_lo):
    x, zh, col, zl, core = (me_ref[k] for k in range(5))

    def left_tile(index, _):
        source = index // 2
        slot = index % 2
        holder = me_ref[5 + PIECES + (2 * col + core) * 8 + first + source]
        owner = (4 * x + zh + holder + 8 * slot + PIECES - col) % PIECES
        dx = ring_place((owner // 4) ^ x, core)
        dz = ring_place((owner % 4) ^ zh, core)
        at = me_ref[5 + 4 * dz + dx]
        lanes = pl.ds(pl.multiple_of(at * LANES, LANES), LANES)
        for r in range(ROWS_A):
            quarter = r // 2
            place = jnp.where(quarter % 2 == core, 2, 0) + jnp.where(quarter // 2 == zl, 1, 0)
            rows = pl.ds(pl.multiple_of(place * 128 + (r % 2) * BLOCK, BLOCK), BLOCK)

            def load(pair):
                return a_f[source, pl.ds(pl.multiple_of((slot * 4 + pair) * BLOCK, BLOCK), BLOCK), :]

            left = spots_s[source, slot * 16 + 2 * r].astype(jnp.int32)
            right = spots_s[source, slot * 16 + 2 * r + 1].astype(jnp.int32)
            a_hi[rows, lanes], a_lo[rows, lanes] = halves(block_pair(load, left, right))
        return 0

    lax.fori_loop(0, 8, left_tile, 0, unroll=4)


def right_copies(call, b_in, b_f, spots_s, sem_b, sem_s):
    tiles = PLACED[call]
    copies, spots = [], []
    for source, held in zip(b_in, [held for held in HELD if set(held) & set(tiles)], strict=True):
        for k, tile in enumerate(held):
            if tile not in tiles:
                continue
            at = tiles.index(tile)
            rows = pl.ds(k * B_ROWS, B_ROWS)
            copies.append(pltpu.make_async_copy(source.at[rows], b_f.at[at], sem_b.at[at]))
            spots.append(pltpu.make_async_copy(source.at[k * B_ROWS + B_DATA], spots_s.at[at], sem_s.at[at]))
    return copies, spots


def place_right(first, tiles, b_f, spots_s, b_hi, b_lo):
    def right_tile(tile, _):
        for k in range(INNER):
            rows = pl.ds(pl.multiple_of(tile * LANES + k * BLOCK, BLOCK), BLOCK)
            for c in range(COLS_B // 2):

                def load(pair):
                    return b_f[first + tile, pl.ds(pl.multiple_of(pair * BLOCK, BLOCK), BLOCK), :]

                spot = k * COLS_B + 2 * c
                left = spots_s[first + tile, spot].astype(jnp.int32)
                right = spots_s[first + tile, spot + 1].astype(jnp.int32)
                lanes = slice(c * LANES, (c + 1) * LANES)
                b_hi[rows, lanes], b_lo[rows, lanes] = halves(block_pair(load, left, right))
        return 0

    lax.fori_loop(0, tiles, right_tile, 0, unroll=3 if tiles % 3 == 0 else 2 - tiles % 2)


def left_copies(parts, a_f, spots_s, sem_a, sem_s):
    copies, spots = [], []
    for n, (part, k) in enumerate([(part, k) for part in parts for k in range(part.shape[0] // A_ROWS)]):
        copies.append(pltpu.make_async_copy(part.at[pl.ds(k * A_ROWS, A_ROWS)], a_f.at[n], sem_a.at[n]))
        spots.append(pltpu.make_async_copy(part.at[k * A_ROWS + A_DATA], spots_s.at[n], sem_s.at[n]))
    return copies, spots


def partial_product(left_hi, left_lo, b_hi, b_lo, store):
    for n in range(4):
        lanes = slice(n * 256, (n + 1) * 256)
        top = b_hi[:, lanes]
        total = jnp.dot(left_lo, top, preferred_element_type=jnp.float32)
        total += jnp.dot(left_hi, b_lo[:, lanes], preferred_element_type=jnp.float32)
        total += jnp.dot(left_hi, top, preferred_element_type=jnp.float32)
        store(lanes, total)


def early_kernel(n_right, *refs):
    b_in = refs[:n_right]
    b_hi, b_lo, ahead_hi, ahead_lo, b_f, spots_b, sem_b, sem_s = refs[n_right:]
    copies, spots = right_copies(0, b_in, b_f, spots_b, sem_b, sem_s)
    for copy in spots + copies:
        copy.start()
    for copy in spots + copies:
        copy.wait()
    place_right(0, len(CALLS[0]), b_f, spots_b, b_hi, b_lo)
    place_right(len(CALLS[0]), 2, b_f, spots_b, ahead_hi, ahead_lo)


def first_kernel(*refs):
    me_ref, a_in, b_in = refs[0], refs[1:4], refs[4:6]
    near_hi, near_lo, c_out = refs[6:9]
    a_f, spots_a, sem_a, sem_sa, b_hi, b_lo, sem_b = refs[9:]
    copies_a, spots_of_a = left_copies(a_in, a_f, spots_a, sem_a, sem_sa)
    copies = [pltpu.make_async_copy(b_in[k], (b_hi, b_lo)[k], sem_b.at[k]) for k in range(2)]
    for copy in spots_of_a + copies_a + copies:
        copy.start()
    for copy in spots_of_a + copies_a:
        copy.wait()
    place_left(me_ref, 0, a_f, spots_a, near_hi, near_lo)
    for copy in copies:
        copy.wait()

    def store(lanes, total):
        c_out[:, lanes] = total

    partial_product(near_hi[:, :FIRST_DEPTH], near_lo[:, :FIRST_DEPTH], b_hi, b_lo, store)


def middle_kernel(n_right, *refs):
    me_ref, a_in, near, c_in, ahead, b_in = refs[0], refs[1], refs[2:4], refs[4], refs[5:7], refs[7 : 7 + n_right]
    late_hi, late_lo, c_out = refs[7 + n_right : 10 + n_right]
    a_f, spots_a, sem_a, sem_sa, c_held, sem_c, b_f, b_hi, b_lo, spots_b, sem_b, sem_s = refs[10 + n_right :]
    copies_a, spots_of_a = left_copies((a_in,), a_f, spots_a, sem_a, sem_sa)
    copies, spots = right_copies(1, b_in, b_f, spots_b, sem_b, sem_s)
    held = [pltpu.make_async_copy(c_in, c_held, sem_c.at[0])]
    for k, dense in enumerate((b_hi, b_lo)):
        held.append(pltpu.make_async_copy(ahead[k], dense.at[pl.ds(0, AHEAD)], sem_c.at[5 + k]))
    for k, late in enumerate((late_hi, late_lo)):
        for n, (first, at, lanes) in enumerate(((FIRST_DEPTH, AHEAD, 256), (FIRST_DEPTH + 256, MIDDLE_DEPTH, 128))):
            source = near[k].at[:, pl.ds(first, lanes)]
            held.append(pltpu.make_async_copy(source, late.at[:, pl.ds(at, lanes)], sem_c.at[1 + 2 * k + n]))
    for copy in spots_of_a + copies_a + spots + copies + held:
        copy.start()
    for copy in spots_of_a + copies_a:
        copy.wait()
    place_left(me_ref, 4, a_f, spots_a, late_hi, late_lo)
    for copy in spots + copies:
        copy.wait()
    rest = pl.ds(AHEAD, MIDDLE_DEPTH - AHEAD)
    place_right(0, len(PLACED[1]), b_f, spots_b, b_hi.at[rest], b_lo.at[rest])
    for copy in held:
        copy.wait()

    def store(lanes, total):
        c_out[:, lanes] = total + c_held[:, lanes]

    partial_product(late_hi[:, :MIDDLE_DEPTH], late_lo[:, :MIDDLE_DEPTH], b_hi, b_lo, store)


def last_kernel(n_right, *refs):
    late_hi, late_lo, c_in = refs[:3]
    b_in = refs[3 : 3 + n_right]
    other, send, keep, b_f, b_hi, b_lo, spots_b, sem_b, sem_s = refs[3 + n_right :]
    copies, spots = right_copies(2, b_in, b_f, spots_b, sem_b, sem_s)
    for copy in spots + copies:
        copy.start()
    for copy in spots + copies:
        copy.wait()
    place_right(0, len(CALLS[2]), b_f, spots_b, b_hi, b_lo)

    def store(lanes, total):
        total += c_in[:, lanes]
        other[:, lanes] = total[:256]
        send[:, lanes] = total[256:384]
        keep[:, lanes] = total[384:]

    partial_product(late_hi[:, MIDDLE_DEPTH:], late_lo[:, MIDDLE_DEPTH:], b_hi, b_lo, store)


def right_scratch(call):
    tiles, depth = len(PLACED[call]), len(CALLS[call]) * LANES
    return [
        pltpu.VMEM((tiles, B_ROWS, LANES), jnp.float32),
        pltpu.VMEM((depth, 1024), jnp.bfloat16),
        pltpu.VMEM((depth, 1024), jnp.bfloat16),
        pltpu.SMEM((tiles, LANES), jnp.float32),
        pltpu.SemaphoreType.DMA((tiles,)),
        pltpu.SemaphoreType.DMA((tiles,)),
    ]


def used_by(call, b_all):
    return [b_all[k] for k in range(len(HELD)) if set(HELD[k]) & set(PLACED[call])]


def cost(call):
    flops = 3 * 2 * 512 * 1024 * LANES * len(CALLS[call])
    return pl.CostEstimate(flops=flops, bytes_accessed=16 * 1024 * 1024, transcendentals=0)


LEFT_SCRATCH = (
    pltpu.VMEM((4, A_ROWS, LANES), jnp.float32),
    pltpu.SMEM((4, LANES), jnp.float32),
    pltpu.SemaphoreType.DMA((4,)),
    pltpu.SemaphoreType.DMA((4,)),
)


def early_right(b_all):
    operands = used_by(0, b_all)
    dense = jax.ShapeDtypeStruct((FIRST_DEPTH, 1024), jnp.bfloat16)
    ahead = jax.ShapeDtypeStruct((AHEAD, 1024), jnp.bfloat16)
    scratch = right_scratch(0)
    return pl.pallas_call(
        lambda *refs: early_kernel(len(operands), *refs),
        out_shape=(dense, dense, ahead, ahead),
        in_specs=[WHERE] * len(operands),
        out_specs=(IN_VMEM,) * 4,
        scratch_shapes=scratch[:1] + scratch[3:],
        compiler_params=pltpu.CompilerParams(vmem_limit_bytes=FIRST),
        cost_estimate=pl.CostEstimate(flops=10**9, bytes_accessed=16 * 1024 * 1024, transcendentals=0),
    )(*operands)


def first_product(me, a_near, right):
    near = jax.ShapeDtypeStruct((512, len(NEAR) * LANES), jnp.bfloat16)
    return pl.pallas_call(
        first_kernel,
        out_shape=(near, near, jax.ShapeDtypeStruct((512, 1024), jnp.float32)),
        in_specs=[IN_SMEM] + [WHERE] * 5,
        out_specs=(IN_VMEM,) * 3,
        scratch_shapes=[*LEFT_SCRATCH, *right_scratch(0)[1:3], pltpu.SemaphoreType.DMA((2,))],
        compiler_params=pltpu.CompilerParams(vmem_limit_bytes=FIRST),
        cost_estimate=cost(0),
    )(me, *a_near, *right)


def middle_product(me, a_far, near_hi, near_lo, so_far, ahead, b_all):
    operands = used_by(1, b_all)
    late = jax.ShapeDtypeStruct((512, len(LATE) * LANES), jnp.bfloat16)
    return pl.pallas_call(
        lambda *refs: middle_kernel(len(operands), *refs),
        out_shape=(late, late, jax.ShapeDtypeStruct((512, 1024), jnp.float32)),
        in_specs=[IN_SMEM] + [WHERE] * (6 + len(operands)),
        out_specs=(IN_VMEM,) * 3,
        scratch_shapes=[
            *LEFT_SCRATCH,
            pltpu.VMEM((512, 1024), jnp.float32),
            pltpu.SemaphoreType.DMA((7,)),
            *right_scratch(1),
        ],
        compiler_params=pltpu.CompilerParams(vmem_limit_bytes=MIDDLE),
        cost_estimate=cost(1),
    )(me, a_far, near_hi, near_lo, so_far, *ahead, *operands)


def last_product(late_hi, late_lo, so_far, b_all):
    operands = used_by(2, b_all)
    return pl.pallas_call(
        lambda *refs: last_kernel(len(operands), *refs),
        out_shape=tuple(jax.ShapeDtypeStruct((rows, 1024), jnp.float32) for rows in (256, 128, 128)),
        in_specs=[IN_VMEM] * 3 + [WHERE] * len(operands),
        out_specs=(IN_VMEM,) * 3,
        scratch_shapes=right_scratch(2),
        compiler_params=pltpu.CompilerParams(vmem_limit_bytes=LAST),
        cost_estimate=cost(2),
    )(late_hi, late_lo, so_far, *operands)


def join_kernel(*refs):
    parts, out, sems = refs[:-2], refs[-2], refs[-1]
    copies, row = [], 0
    for k, part in enumerate(parts):
        copies.append(pltpu.make_async_copy(part, out.at[pl.ds(row, part.shape[0])], sems.at[k]))
        row += part.shape[0]
    for copy in copies:
        copy.start()
    for copy in copies:
        copy.wait()


def join(parts):
    rows = sum(part.shape[0] for part in parts)
    return pl.pallas_call(
        join_kernel,
        out_shape=jax.ShapeDtypeStruct((rows, LANES), jnp.float32),
        in_specs=[WHERE] * len(parts),
        out_specs=IN_VMEM,
        scratch_shapes=[pltpu.SemaphoreType.DMA((len(parts),))],
        compiler_params=pltpu.CompilerParams(vmem_limit_bytes=4 * 1024 * 1024),
    )(*parts)


def body(a_values, a_places, a_counts, b_values, b_places, b_counts):
    hold = lax.optimization_barrier
    by_place = [holder for place in range(8) for core in range(2) for holder in holders(place, core)]
    me = [lax.axis_index(name) for name in ("x", "zh", "col", "zl", "core")]
    table = jnp.array([(NEAR if tile in NEAR else LATE).index(tile) for tile in range(PIECES)] + by_place, jnp.int32)
    me = jnp.concatenate([jnp.stack(me).astype(jnp.int32), table])
    own_a, own = pack(
        a_counts.reshape(2),
        b_counts,
        a_places.reshape(2, CAP_A, 2).swapaxes(1, 2),
        b_places.reshape(CAP_B, 2).swapaxes(0, 1),
        b_values.reshape(CAP_B, BLOCK, BLOCK),
        a_values.reshape(2 * CAP_A, BLOCK, BLOCK),
    )
    z_one = exchange(own, "zh", 0)
    x_one = exchange(own, "x", 0)
    z_one, own_a, me = hold((z_one, own_a, me))
    a_one = exchange_col(own_a, 4)

    z_two = exchange(jnp.concatenate([own, z_one, own[:8]], axis=0), "zh", 1)
    x_two = exchange(jnp.concatenate([own, x_one], axis=0), "x", 1)
    x_two, z_two = hold((x_two, z_two))
    a_one, _ = hold((a_one, z_two))
    a_two = exchange_col(jnp.concatenate([own_a, a_one], axis=0), 2)

    column = jnp.concatenate([z_one, z_two[: 2 * B_ROWS]], axis=0)
    x_three = exchange(column, "x", 0)
    x_four = exchange(column, "x", 1)
    b_all = [own, z_one, x_one, z_two, x_two]
    right = early_right(b_all)
    a_two, *right = hold((a_two, *right))
    a_four = exchange_col(join([own_a, a_one, a_two]), 1)
    x_three, a_two = hold((x_three, a_two))
    near_hi, near_lo, total = first_product(me, (own_a, a_one, a_two), right[:2])
    b_all += [x_three, x_four, exchange(x_three, "x", 1)]
    late_hi, late_lo, total = middle_product(me, a_four, near_hi, near_lo, total, right[2:], b_all)
    other, send, keep = last_product(late_hi, late_lo, total, b_all)

    got = swap(other, "core")
    ahead = swap(send + got[:128], "zl")
    return (keep + got[128:]) + ahead


def solution(mesh):
    split = Mesh(mesh.devices.reshape(4, 4, 8, 2, 2), ("x", "zh", "col", "zl", "core"))
    row, layer = ("x", "zh"), ("zl", "core")
    in_specs = (
        P(row, "col", layer, None, None, None, None),
        P(row, "col", layer, None, None, None),
        P(row, "col", layer, None),
        P(row, "col", layer, None, None, None),
        P(row, "col", layer, None, None),
        P(row, "col", layer),
    )
    out_specs = P(("x", "zh", "zl", "core"), "col")
    return jax.shard_map(body, mesh=split, in_specs=in_specs, out_specs=out_specs, check_vma=False)
```
